512 devices in a mesh: freq: 8 (over x, core), tile: 64 (over z, y).
Axes of the slice: x: 4, y: 4, z: 16, core: 2. Of those that a mesh axis runs over, the one named last changes fastest.
Arguments:
- left_basis: bfloat16 [16, 8192, 2, 1536], P('freq', 'tile'), may hold values from -0.078125 to 0.078125
- right_basis: bfloat16 [16, 8192, 2, 1536], P('freq', 'tile'), may hold values from -0.25 to 0.25
- start_model: float32 [16, 8192, 128], P('freq', 'tile'), may hold values from -3 to 3
- recorded: float32 [16, 8192, 128], P('freq', 'tile'), may hold values from -6 to 6
- tile_ranks: int32 [16, 16], replicated, may hold values from 16 to 96, as said below
- mute_start: int32 [8192, 64], P('tile'), may hold values from 0 to 127
- thresholds: float32 [64], replicated, may hold values from 0.05 to 0.5
Outputs:
- estimate: float32 [16, 8192, 128], P('freq', 'tile')
- misfit: float32 [16, 8192, 128], P('freq', 'tile')
The draws below stay inside these ranges and needn't reach their ends.
Inputs may be any that keep to these rules, and one draw needn't show every extreme that they name: `tile_ranks`: some tile has rank 96 and some rank 16.
All inputs are finite; a program needn't handle non-finite values.
Results may differ from the reference program's by a relative error of at most 0.013.
Values may be sent and summed in bfloat16 or wider, within the bound.
A program may use at most 64 MiB of HBM per device.

```python
import math
import jax
import jax.numpy as jnp
from jax import lax

NB = 512
TSIDE = 16
N = 8192
RMAX = 96
RMIN = 16
S = 64
NF = 16
NT = 256
GROUP = 4
OUTER = 2
INNER = 1


def draw_tile_ranks(key, part):
    first_key, second_key = jax.random.split(jax.random.fold_in(key, 7))
    values = jax.random.randint(first_key, (TSIDE * TSIDE,), RMIN, RMAX + 1)
    spots = jax.random.permutation(second_key, TSIDE * TSIDE)
    values = values.at[spots[0]].set(RMAX).at[spots[1]].set(RMIN)
    return values.reshape(TSIDE, TSIDE).astype(jnp.int32)


def place_ends(entries, stream_key, low, largest):
    spot = [jax.random.randint(jax.random.fold_in(stream_key, axis), (), 0, length) for axis, length in enumerate(entries.shape)]
    widest = entries.shape.index(max(entries.shape))
    beside = spot[:widest] + [(spot[widest] + 1) % entries.shape[widest]] + spot[widest + 1:]
    return entries.at[tuple(spot)].set(low).at[tuple(beside)].set(largest)


def block_scale(own_key, extent, pieces, least, top_value):
    level, own = 1.0, jax.random.fold_in(own_key, 6)
    for position, blocks in pieces:
        heights = jnp.exp(jax.random.uniform(jax.random.fold_in(own, position), (blocks,), jnp.float32, least / len(pieces), top_value / len(pieces)))
        level = level * jnp.repeat(heights, extent[position] // blocks).reshape([-1 if axis == position else 1 for axis in range(len(extent))])
    return level


def normal_values(own_key, shape, deviation, limit, shards=(), held_as=jnp.bfloat16):
    drawn = jax.random.normal(own_key, shape, jnp.float32) * deviation
    if len(shards) > 0:
        drawn = block_scale(own_key, shape, shards, -0.22, 0.18) * drawn
    return jnp.clip(drawn, min=-limit, max=limit).astype(held_as)


def setup_inputs(seed: int = 0) -> dict:
    keys = jax.random.split(jax.random.key(seed), 8)
    return {
        "left_basis": normal_values(keys[0], (NF, N, 2, TSIDE * RMAX), (4 * TSIDE * RMAX) ** -0.5, 0.078125, ((0, 8), (1, 64))),
        "right_basis": normal_values(keys[1], (NF, N, 2, TSIDE * RMAX), NB ** -0.5, 0.25, ((0, 8), (1, 64))),
        "start_model": normal_values(keys[2], (NF, N, 2 * S), 0.5, 3.0, ((0, 8), (1, 64)), jnp.float32),
        "recorded": normal_values(keys[3], (NF, N, 2 * S), 1.0, 6.0, ((0, 8), (1, 64)), jnp.float32),
        "tile_ranks": draw_tile_ranks(jax.random.fold_in(keys[7], 71), 0),
        "mute_start": place_ends(jax.random.randint(keys[5], (N, S), 0, NT // 2), jax.random.fold_in(keys[5], 1), 0, (NT // 2) - 1).astype(jnp.int32),
        "thresholds": jnp.clip(jnp.exp(jax.random.uniform(keys[6], (S,), jnp.float32, math.log(0.05), math.log(0.5))), 0.05, 0.5),
    }


STEP_SIZE = 0.5

def phase_table():
    sample_index = jnp.arange(NT, dtype=jnp.int32)[:, None]
    bin_index = jnp.arange(NF, dtype=jnp.int32)[None, :] + NT // 4
    phases = (sample_index * bin_index % NT).astype(jnp.float32) * (2.0 * math.pi / NT)
    return jnp.stack([jnp.cos(phases), -jnp.sin(phases)])

def coefficients(basis, vector, rank_mask):
    sub_rows = N // TSIDE // GROUP
    blocks = basis.reshape(TSIDE, GROUP, sub_rows, 2, TSIDE * RMAX)
    vectors = vector.reshape(TSIDE, GROUP, sub_rows, 2 * S)

    def per_block(operands):
        tile_block, values, kept_mask = operands
        product = jnp.einsum('gnak,gnc->gakc', tile_block.astype(jnp.float32), values.astype(jnp.float32))
        real_part = product[:, 0, :, :S] + product[:, 1, :, S:]
        imag_part = product[:, 0, :, S:] - product[:, 1, :, :S]
        partial_value = jnp.concatenate([real_part, imag_part], 2).reshape(GROUP, TSIDE, RMAX, 2 * S)
        partial_value = partial_value * kept_mask[None, :, :, None]
        partial_value = lax.optimization_barrier(partial_value.astype(jnp.bfloat16)).astype(jnp.float32)
        return lax.optimization_barrier(jnp.sum(partial_value, 0)).astype(jnp.bfloat16)
    return lax.map(per_block, (blocks, vectors, rank_mask))

def expand(basis, coefficient):
    blocks = basis.reshape(TSIDE, N // TSIDE, 2, TSIDE * RMAX)

    def per_block(operands):
        tile_block, values = operands
        product = jnp.einsum('nak,kc->nac', tile_block.astype(jnp.float32), values.reshape(TSIDE * RMAX, 2 * S).astype(jnp.float32))
        real_part = product[:, 0, :S] - product[:, 1, S:]
        imag_part = product[:, 0, S:] + product[:, 1, :S]
        return jnp.concatenate([real_part, imag_part], 1)
    return lax.map(per_block, (blocks, coefficient)).reshape(N, 2 * S)

def sparsify(estimate, mute_start, thresholds):
    wave_table = phase_table()
    stacked = estimate.reshape(NF, N, 2, S)
    series = jnp.einsum('atk,knas->nst', wave_table, stacked, precision=lax.Precision.HIGHEST) / math.sqrt(NF)
    sample_index = jnp.arange(NT, dtype=jnp.int32)
    series = jnp.where(sample_index[None, None, :] >= mute_start[:, :, None], series, jnp.zeros_like(series))
    cutoff = thresholds[None, :, None]
    series = series - jnp.clip(series, -cutoff, cutoff)
    returned = jnp.einsum('nst,atk->knas', series, wave_table, precision=lax.Precision.HIGHEST) * (2.0 * math.sqrt(NF) / NT)
    return returned.reshape(NF, N, 2 * S)

def reference(left_basis, right_basis, start_model, recorded, tile_ranks, mute_start, thresholds):
    levels = jnp.arange(RMAX, dtype=jnp.int32)
    left_mask = (levels[None, None, :] < tile_ranks[:, :, None]).astype(jnp.float32)
    right_mask = jnp.transpose(left_mask, (1, 0, 2))

    def per_frequency(operands):
        left_one, right_one, estimate_one, recorded_one = operands
        forward = coefficients(right_one, estimate_one.astype(jnp.bfloat16), right_mask)
        misfit_one = expand(left_one, jnp.transpose(forward, (1, 0, 2, 3))) - recorded_one
        adjoint = coefficients(left_one, misfit_one.astype(jnp.bfloat16), left_mask)
        gradient = expand(right_one, jnp.transpose(adjoint, (1, 0, 2, 3)))
        return (estimate_one - STEP_SIZE * gradient, misfit_one)
    estimate = start_model
    misfit = recorded
    for outer_step in range(OUTER):
        for inner_step in range(INNER):
            estimate, misfit = lax.map(per_frequency, (left_basis, right_basis, estimate, recorded))
        estimate = sparsify(estimate, mute_start, thresholds)
    return (estimate, misfit)
```

```python
import math

import jax
import jax.numpy as jnp
import ml_dtypes
import numpy as np
from jax import lax
from jax.experimental import pallas as pl
from jax.experimental.pallas import tpu as pltpu
from jax.sharding import PartitionSpec as P

F32 = jnp.float32
BF16 = jnp.bfloat16
NT = 256
NF = 16
STEP_SIZE = 0.5


def split_table(table, terms):
    parts = []
    rest = table
    for _ in range(terms):
        part = rest.astype(ml_dtypes.bfloat16)
        parts.append(part)
        rest = rest - part.astype(np.float64)
    return parts


def wave_tables():
    sample = np.arange(NT)[:, None]
    bins = np.arange(NF)[None, :] + NT // 4
    phases = (sample * bins % NT) * (2.0 * math.pi / NT)
    table = np.concatenate([np.cos(phases), -np.sin(phases)], 1)
    forward = np.concatenate(split_table(table, 3), 1)
    backward = np.concatenate(split_table(np.ascontiguousarray(table.T), 2), 0)
    return forward, backward


def kernel(
    left, right, model0, recorded, ranks, mute, thresholds, wave, wave_back,
    estimate_out, misfit_out,
    left_rows, right_rows, left_cols, right_cols,
    model_full, model_half, recorded_half, packed, weights, product,
    outbox, inbox, own_sum, sib_sum, misfit_full,
    spread_out, spread_in, spread_f32, traces, traces_b, mute_rows,
    basis_s, basis_r, init_s, init_r, fwd_s, fwd_r, z_s, z_r, ex_s, ex_r,
    sp_s, sp_r, back_s, back_r, fin_s, fin_r, mis_s, mis_r,
):
    freq_id = lax.axis_index("freq")
    tile_id = lax.axis_index("tile")
    x, c = freq_id // 2, freq_id % 2
    z, y = tile_id // 4, tile_id % 4
    pair = z // 8
    me = (x, c, z, y)

    def address(place):
        return (place[0] * 2 + place[1], place[2] * 4 + place[3])

    def is_me(place):
        to = address(place)
        return jnp.logical_and(to[0] == freq_id, to[1] == tile_id)

    def remote(src, dst, send_sem, recv_sem, place):
        return pltpu.make_async_remote_copy(
            src_ref=src, dst_ref=dst, send_sem=send_sem, recv_sem=recv_sem,
            device_id=address(place), device_id_type=pl.DeviceIdType.MESH,
        )

    def send(src, dst, send_sem, recv_sem, place):
        mine = is_me(place)

        @pl.when(jnp.logical_not(mine))
        def _():
            remote(src, dst, send_sem, recv_sem, place).start()

        @pl.when(mine)
        def _():
            pltpu.make_async_copy(src, dst, recv_sem).start()

    def sent(src, dst, send_sem, recv_sem, place):
        @pl.when(jnp.logical_not(is_me(place)))
        def _():
            remote(src, dst, send_sem, recv_sem, place).wait_send()

    def arrived(ref, sem):
        pltpu.make_async_copy(ref, ref, sem).wait()

    barrier = pltpu.get_barrier_semaphore()

    def greet(place):
        pl.semaphore_signal(
            barrier, inc=1, device_id=address(place), device_id_type=pl.DeviceIdType.MESH
        )

    def greet_plane(index, carry):
        place = (index // 8, (index // 4) % 2, z, index % 4)

        @pl.when(jnp.logical_not(is_me(place)))
        def _():
            greet(place)
        return carry

    def greet_line(index, carry):
        @pl.when(8 * c + index != z)
        def _():
            greet((x, pair, 8 * c + index, y))
        return carry

    lax.fori_loop(0, 32, greet_plane, 0)
    lax.fori_loop(0, 8, greet_line, 0)
    pl.semaphore_wait(barrier, 39 - (pair == c).astype(jnp.int32))

    def basis_copy(which, t, q):
        source = (right, left)[which]
        rows = (right_rows, left_rows)[which]
        side, l = q // 2, q % 2
        return (
            source.at[l, :, 6 * side + t],
            rows.at[t, pl.ds(128 * y, 128)],
            basis_s.at[which, 4 * t + q],
            basis_r.at[which, t],
            (x, side, z, 2 * c + l),
        )

    def send_basis(which, t):
        def one(q, carry):
            send(*basis_copy(which, t, q))
            return carry
        lax.fori_loop(0, 4, one, 0)

    def init_copies(l):
        place = (x, y // 2, z, 2 * c + l)
        return (
            (model0.at[l], model_half.at[y % 2], init_s.at[l], init_r.at[0], place),
            (recorded.at[l], recorded_half.at[y % 2], init_s.at[2 + l], init_r.at[1], place),
        )

    for l in range(2):
        send(*init_copies(l)[0])
    for t in range(6):
        send_basis(0, t)
    for l in range(2):
        send(*init_copies(l)[1])

    sibling = (x, 1 - c, z, y)
    lane = lax.broadcasted_iota(jnp.int32, (1, 128), 1)
    low = lane < 64
    sign = jnp.where(low, 1.0, -1.0).astype(F32)

    mute_t = mute[...].astype(F32).T
    mute_rows[...] = jnp.concatenate([mute_t, mute_t], 1)
    first_row = pl.multiple_of(32 * x + 16 * c, 16)
    window = jnp.where(
        low, mute_rows[pl.ds(first_row, 8, stride=2), :], mute_rows[pl.ds(first_row + 1, 8, stride=2), :]
    )
    cutoff = jnp.concatenate([thresholds[...], thresholds[...]], 1)

    def set_weights(block, values):
        values = values.astype(BF16).astype(F32)
        packed[pl.ds(0, 128, stride=2), :] = values
        packed[pl.ds(1, 128, stride=2), :] = pltpu.roll(values, 64, 1) * sign
        weights[256 * block:256 * block + 256, :] = packed[...].astype(BF16)

    slots = lax.broadcasted_iota(jnp.int32, (96, 128), 0)

    def z_copy(step, s):
        return (
            outbox.at[step, s], inbox.at[step, z % 8], z_s.at[step, s], z_r.at[step, z % 8],
            (x, pair, 8 * c + s, y),
        )

    def partials(step, cols, h):
        values = jnp.dot(
            cols[384 * h:384 * h + 384, :], weights[...], preferred_element_type=F32
        )
        for s4 in range(4):
            s = 4 * h + s4
            other = 8 * c + s
            rank = ranks[other, z] if step % 2 == 0 else ranks[z, other]
            part = values[96 * s4:96 * s4 + 96, :]
            outbox[step, s] = jnp.where(slots < rank, part, 0.0).astype(BF16)
            send(*z_copy(step, s))

    def transpose(rows, cols, t):
        cols[128 * t:128 * t + 128, :] = rows.reshape(6, 1024, 128)[t].T

    def expand(rows, step, block):
        start = 256 * block if isinstance(block, int) else pl.multiple_of(256 * block, 256)
        view = rows.reshape(6, 1024, 128)
        lhs = jnp.concatenate([view[t, pl.ds(start, 256), :] for t in range(6)], 1)
        rhs = inbox[step].reshape(768, 128)
        product[...] = jnp.dot(lhs, rhs, preferred_element_type=F32)
        real = product[pl.ds(0, 128, stride=2), :]
        imag = product[pl.ds(1, 128, stride=2), :]
        return real - pltpu.roll(imag, 64, 1) * sign

    def exchange(step, block, slot):
        return remote(
            own_sum.at[step, block], sib_sum.at[step, slot], ex_s.at[step, slot],
            ex_r.at[step, slot], sibling,
        )

    def receive_line(step):
        for s in range(8):
            arrived(inbox.at[step, s], z_r.at[step, s])

    def residual(step):
        receive_line(step)
        for block in range(4):
            part = expand(left_rows, step, block)
            kept = jnp.where(block // 2 == c, recorded_half[block % 2], 0.0)
            own_sum[step, block] = part - kept
            exchange(step, block, block).start()
        for block in range(4):
            exchange(step, block, block).wait_recv()
            values = own_sum[step, block] + sib_sum[step, block]
            if step == 2:
                misfit_full[block] = values
            set_weights(block, values)

    def update(step):
        receive_line(step)
        for q in range(2):
            block = 2 * (1 - c) + q
            own_sum[step, block] = expand(right_rows, step, block)
            exchange(step, block, q).start()
        for q in range(2):
            own_sum[step, 2 * c + q] = expand(right_rows, step, 2 * c + q)
        for q in range(2):
            exchange(step, 2 * (1 - c) + q, q).wait_recv()
            total = own_sum[step, 2 * c + q] + sib_sum[step, q]
            model_half[q] = model_half[q] - STEP_SIZE * total

    def spread_copy(outer, index):
        q, column, core = index // 8, (index // 2) % 4, index % 2
        return (
            spread_out.at[outer, q, pl.ds(pl.multiple_of(32 * column + 16 * core, 16), 16)],
            spread_in.at[outer, 4 * x + y],
            sp_s.at[outer, index], sp_r.at[outer],
            (column, core, z, 2 * c + q),
        )

    def sparsify(outer):
        spread_out[outer] = model_half[...].astype(BF16)

        def one(index, carry):
            send(*spread_copy(outer, index))
            return carry
        lax.fori_loop(0, 16, one, 0)
        arrived(spread_in.at[outer], sp_r.at[outer])
        spread_f32[...] = spread_in[outer].reshape(256, 128).astype(F32)
        flat = traces.reshape(256, 128)
        sample = lax.broadcasted_iota(jnp.int32, (NT, 128), 0).astype(F32)
        for p in range(8):
            even = spread_f32[pl.ds(2 * p, 16, stride=16), :]
            odd = spread_f32[pl.ds(2 * p + 1, 16, stride=16), :]
            real = jnp.where(low, even, pltpu.roll(odd, 64, 1))
            imag = jnp.where(low, pltpu.roll(even, 64, 1), odd)
            both = jnp.concatenate([real, imag], 0).astype(BF16)
            series = jnp.dot(
                wave[...], jnp.concatenate([both, both, both], 0), preferred_element_type=F32
            ) * (1.0 / math.sqrt(NF))
            series = jnp.where(sample >= window[p:p + 1, :], series, 0.0)
            series = series - jnp.clip(series, -cutoff, cutoff)
            high = series.astype(BF16)
            rest = (series - high.astype(F32)).astype(BF16)
            first = jnp.dot(wave_back[...], high, preferred_element_type=F32)
            second = jnp.dot(wave_back[0:32, :], rest, preferred_element_type=F32)
            returned = (first[0:32] + first[32:64] + second) * (2.0 * math.sqrt(NF) / NT)
            real, imag = returned[0:16], returned[16:32]
            flat[pl.ds(2 * p, 16, stride=16), :] = jnp.where(low, real, pltpu.roll(imag, 64, 1))
            flat[pl.ds(2 * p + 1, 16, stride=16), :] = jnp.where(low, pltpu.roll(real, 64, 1), imag)

    def back_copy(index):
        owner, core = index // 2, index % 2
        return (
            traces_b.at[owner],
            model_full.at[pl.ds(pl.multiple_of(128 * y + 32 * x + 16 * c, 16), 16)],
            back_s.at[index], back_r.at[0],
            (owner // 4, core, z, owner % 4),
        )

    def final_copy(index):
        return (
            traces.at[pl.ds(2 * index, 2)],
            estimate_out.at[:, pl.ds(pl.multiple_of(32 * x + 16 * c, 16), 16)],
            fin_s.at[index], fin_r.at[0],
            (index // 2, index % 2, z, y),
        )

    def misfit_copy(q):
        return (
            misfit_full.at[2 * c + q], misfit_out.at[y % 2], mis_s.at[q], mis_r.at[0],
            (x, y // 2, z, 2 * c + q),
        )

    arrived(model_half, init_r.at[0])
    forward = remote(model_half, sib_sum.at[3, pl.ds(2, 2)], fwd_s.at[0], fwd_r.at[0], sibling)
    forward.start()
    forward.wait_recv()
    for block in range(4):
        mine = model_half[block % 2]
        theirs = sib_sum[3, 2 + block % 2]
        set_weights(block, jnp.where(block // 2 == c, mine, theirs))

    for t in range(6):
        arrived(right_rows.at[t], basis_r.at[0, t])
        send_basis(1, t)
        transpose(right_rows, right_cols, t)
        if t % 3 == 2:
            partials(0, right_cols, t // 3)
    for t in range(6):
        arrived(left_rows.at[t], basis_r.at[1, t])
        transpose(left_rows, left_cols, t)
    arrived(recorded_half, init_r.at[1])
    forward.wait_send()

    for outer in range(2):
        if outer == 1:
            partials(2, right_cols, 0)
            partials(2, right_cols, 1)
        residual(2 * outer)
        partials(2 * outer + 1, left_cols, 0)
        partials(2 * outer + 1, left_cols, 1)
        if outer == 1:
            for q in range(2):
                send(*misfit_copy(q))
        update(2 * outer + 1)
        sparsify(outer)
        if outer == 0:
            traces_b[...] = traces[...].astype(BF16)

            def back_one(index, carry):
                send(*back_copy(index))
                return carry
            lax.fori_loop(0, 32, back_one, 0)
            arrived(model_full, back_r.at[0])
            for block in range(4):
                set_weights(block, model_full[128 * block:128 * block + 128, :].astype(F32))
            for q in range(2):
                rows = pl.ds(pl.multiple_of(256 * c + 128 * q, 128), 128)
                model_half[q] = model_full[rows, :].astype(F32)

    def final_one(index, carry):
        send(*final_copy(index))
        return carry
    lax.fori_loop(0, 8, final_one, 0)

    def basis_done(index, carry):
        for which in range(2):
            sent(*basis_copy(which, index // 4, index % 4))
        return carry
    lax.fori_loop(0, 24, basis_done, 0)
    for l in range(2):
        for item in init_copies(l):
            sent(*item)
        sent(*misfit_copy(l))
    for step in range(4):
        def z_done(s, carry):
            sent(*z_copy(step, s))
            return carry
        lax.fori_loop(0, 8, z_done, 0)
        if step % 2 == 0:
            for block in range(4):
                exchange(step, block, block).wait_send()
        else:
            for q in range(2):
                exchange(step, 2 * (1 - c) + q, q).wait_send()

    def spread_done(index, carry):
        for outer in range(2):
            sent(*spread_copy(outer, index))
        return carry
    lax.fori_loop(0, 16, spread_done, 0)

    def back_done(index, carry):
        sent(*back_copy(index))
        return carry
    lax.fori_loop(0, 32, back_done, 0)

    def final_done(index, carry):
        sent(*final_copy(index))
        return carry
    lax.fori_loop(0, 8, final_done, 0)
    arrived(misfit_out, mis_r.at[0])
    arrived(estimate_out, fin_r.at[0])


def body(left_basis, right_basis, start_model, recorded, tile_ranks, mute_start, thresholds):
    def lanes(basis):
        return basis.reshape(2, 128, 2, 12, 128).transpose(0, 1, 3, 2, 4)

    wave, wave_back = wave_tables()
    anywhere = pl.BlockSpec(memory_space=pl.ANY)
    vmem = pl.BlockSpec(memory_space=pltpu.VMEM)
    dma = pltpu.SemaphoreType.DMA
    field = jax.ShapeDtypeStruct((2, 128, 128), F32)
    return pl.pallas_call(
        kernel,
        out_shape=(field, field),
        in_specs=[anywhere] * 4 + [pl.BlockSpec(memory_space=pltpu.SMEM)] + [vmem] * 4,
        out_specs=(vmem, vmem),
        scratch_shapes=[
            pltpu.VMEM((6, 512, 2, 128), BF16),
            pltpu.VMEM((6, 512, 2, 128), BF16),
            pltpu.VMEM((768, 1024), BF16),
            pltpu.VMEM((768, 1024), BF16),
            pltpu.VMEM((512, 128), BF16),
            pltpu.VMEM((2, 128, 128), F32),
            pltpu.VMEM((2, 128, 128), F32),
            pltpu.VMEM((256, 128), F32),
            pltpu.VMEM((1024, 128), BF16),
            pltpu.VMEM((256, 128), F32),
            pltpu.VMEM((4, 8, 96, 128), BF16),
            pltpu.VMEM((4, 8, 96, 128), BF16),
            pltpu.VMEM((4, 4, 128, 128), F32),
            pltpu.VMEM((4, 4, 128, 128), F32),
            pltpu.VMEM((4, 128, 128), F32),
            pltpu.VMEM((2, 2, 128, 128), BF16),
            pltpu.VMEM((2, 16, 16, 128), BF16),
            pltpu.VMEM((256, 128), F32),
            pltpu.VMEM((16, 16, 128), F32),
            pltpu.VMEM((16, 16, 128), BF16),
            pltpu.VMEM((128, 128), F32),
            dma((2, 24)), dma((2, 6)), dma((4,)), dma((2,)), dma((1,)), dma((1,)),
            dma((4, 8)), dma((4, 8)), dma((4, 4)), dma((4, 4)),
            dma((2, 16)), dma((2,)), dma((32,)), dma((1,)), dma((8,)), dma((1,)), dma((2,)), dma((1,)),
        ],
        compiler_params=pltpu.CompilerParams(
            collective_id=0, has_side_effects=True, vmem_limit_bytes=40 * 1024 * 1024
        ),
    )(
        lanes(left_basis), lanes(right_basis), start_model, recorded, tile_ranks,
        mute_start.T, thresholds.reshape(1, 64), jnp.asarray(wave), jnp.asarray(wave_back),
    )


def solution(mesh):
    return jax.shard_map(
        body,
        mesh=mesh,
        in_specs=(
            P("freq", "tile", None, None),
            P("freq", "tile", None, None),
            P("freq", "tile", None),
            P("freq", "tile", None),
            P(),
            P("tile", None),
            P(),
        ),
        out_specs=(P("freq", "tile", None), P("freq", "tile", None)),
        check_vma=False,
    )
```

```python
import math

import jax
import jax.numpy as jnp
import ml_dtypes
import numpy as np
from jax import lax
from jax.experimental import pallas as pl
from jax.experimental.pallas import tpu as pltpu
from jax.sharding import PartitionSpec as P

F32 = jnp.float32
BF16 = jnp.bfloat16
NT = 256
NF = 16
STEP_SIZE = 0.5
PLANE = sorted(
    ((dx, dy) for dx in range(4) for dy in range(4)),
    key=lambda o: (-min(o[0], 4 - o[0]) - min(o[1], 4 - o[1]), o),
)


def split_table(table, terms):
    parts = []
    rest = table
    for _ in range(terms):
        part = rest.astype(ml_dtypes.bfloat16)
        parts.append(part)
        rest = rest - part.astype(np.float64)
    return parts


def wave_tables():
    sample = np.arange(NT)[:, None]
    bins = np.arange(NF)[None, :] + NT // 4
    phases = (sample * bins % NT) * (2.0 * math.pi / NT)
    table = np.concatenate([np.cos(phases), -np.sin(phases)], 1)
    forward = np.concatenate(split_table(table, 3), 1)
    backward = np.concatenate(split_table(np.ascontiguousarray(table.T), 2), 0)
    return forward, backward


def kernel(
    left, right, model0, recorded, ranks, mute_in, thresholds_in, wave_in, wave_back_in,
    estimate_out, misfit_out,
    left_rows, right_rows, left_cols, right_cols,
    model_full, model_half, recorded_half, packed, weights, product,
    outbox, inbox, own_sum, sib_sum, misfit_full,
    spread_out, spread_in, spread_f32, traces, traces_b, mute_rows,
    mute, thresholds, wave, wave_back, small_s,
    local_rows, local_model, local_weights, group_out, group_in, local_r, group_s, group_r,
    basis_s, basis_r, init_s, init_r, z_s, z_r, ex_s, ex_r,
    sp_s, sp_r, back_s, back_r, fin_s, fin_r, mis_s, mis_r,
):
    freq_id = lax.axis_index("freq")
    tile_id = lax.axis_index("tile")
    x, c = freq_id // 2, freq_id % 2
    z, y = tile_id // 4, tile_id % 4
    pair = z // 8
    me = (x, c, z, y)

    def address(place):
        return (place[0] * 2 + place[1], place[2] * 4 + place[3])

    def is_me(place):
        to = address(place)
        return jnp.logical_and(to[0] == freq_id, to[1] == tile_id)

    def remote(src, dst, send_sem, recv_sem, place):
        return pltpu.make_async_remote_copy(
            src_ref=src, dst_ref=dst, send_sem=send_sem, recv_sem=recv_sem,
            device_id=address(place), device_id_type=pl.DeviceIdType.MESH,
        )

    def send(src, dst, send_sem, recv_sem, place, may_be_me=True):
        if not may_be_me:
            remote(src, dst, send_sem, recv_sem, place).start()
            return
        mine = is_me(place)

        @pl.when(jnp.logical_not(mine))
        def _():
            remote(src, dst, send_sem, recv_sem, place).start()

        @pl.when(mine)
        def _():
            pltpu.make_async_copy(src, dst, recv_sem).start()

    def sent(src, dst, send_sem, recv_sem, place, may_be_me=True):
        if not may_be_me:
            remote(src, dst, send_sem, recv_sem, place).wait_send()
            return

        @pl.when(jnp.logical_not(is_me(place)))
        def _():
            remote(src, dst, send_sem, recv_sem, place).wait_send()

    def arrived(ref, sem):
        pltpu.make_async_copy(ref, ref, sem).wait()

    barrier = pltpu.get_barrier_semaphore()

    def greet(place):
        pl.semaphore_signal(
            barrier, inc=1, device_id=address(place), device_id_type=pl.DeviceIdType.MESH
        )

    small = [
        pltpu.make_async_copy(src, dst, small_s.at[i])
        for i, (src, dst) in enumerate(
            ((mute_in, mute), (thresholds_in, thresholds), (wave_in, wave), (wave_back_in, wave_back))
        )
    ]

    def greet_line(index, carry):
        @pl.when(8 * c + index != z)
        def _():
            greet((x, pair, 8 * c + index, y))
        return carry

    local_model_copy = pltpu.make_async_copy(model0, local_model, local_r.at[4])
    local_model_copy.start()

    def local_load(h):
        for l in range(2):
            for side in range(2):
                for t3 in range(3):
                    t = 6 * side + 3 * h + t3
                    pltpu.make_async_copy(
                        right.at[l, :, t], local_rows.at[l, 3 * (2 * h + side) + t3], local_r.at[2 * h + l]
                    ).start()

    local_load(0)
    local_load(1)
    lax.fori_loop(0, 8, greet_line, 0)
    for dx, dy in PLANE:
        for dc in (1, 0):
            if (dx, dy, dc) != (0, 0, 0):
                greet(((x + dx) % 4, (c + dc) % 2, z, (y + dy) % 4))
    for copy in small:
        copy.start()

    def basis_copy(which, t, q):
        source = (right, left)[which]
        rows = (right_rows, left_rows)[which]
        side, l = q // 2, q % 2
        return (
            source.at[l, :, 6 * side + t],
            rows.at[t, pl.ds(128 * y, 128)],
            basis_s.at[which, 4 * t + q],
            basis_r.at[which, t],
            (x, side, z, 2 * c + l),
        )

    def send_basis(which, t):
        def one(q, carry):
            send(*basis_copy(which, t, q))
            return carry
        lax.fori_loop(0, 4, one, 0)

    def init_copies(l):
        place = (x, y // 2, z, 2 * c + l)
        return (
            (model0.at[l], model_half.at[y % 2], init_s.at[l], init_r.at[0], place),
            (recorded.at[l], recorded_half.at[y % 2], init_s.at[2 + l], init_r.at[1], place),
        )

    sibling = (x, 1 - c, z, y)
    lane = lax.broadcasted_iota(jnp.int32, (1, 128), 1)
    low = lane < 64
    sign = jnp.where(low, 1.0, -1.0).astype(F32)

    def interleave(values):
        values = values.astype(BF16).astype(F32)
        packed[pl.ds(0, 128, stride=2), :] = values
        packed[pl.ds(1, 128, stride=2), :] = pltpu.roll(values, 64, 1) * sign
        return packed[...].astype(BF16)

    def set_weights(block, values):
        weights[256 * block:256 * block + 256, :] = interleave(values)

    slots = lax.broadcasted_iota(jnp.int32, (96, 128), 0)

    def z_copy(step, s):
        return (
            outbox.at[step, s], inbox.at[step, z % 8], z_s.at[step, s], z_r.at[step, z % 8],
            (x, pair, 8 * c + s, y),
        )

    def fill_outbox(step, h, values):
        for s4 in range(4):
            s = 4 * h + s4
            other = 8 * c + s
            rank = ranks[other, z] if step % 2 == 0 else ranks[z, other]
            part = values[96 * s4:96 * s4 + 96, :]
            outbox[step, s] = jnp.where(slots < rank, part, 0.0).astype(BF16)
            if step == 0:
                send(*z_copy(step, s))

    def partials(step, cols, h):
        fill_outbox(
            step, h,
            jnp.dot(cols[384 * h:384 * h + 384, :], weights[...], preferred_element_type=F32),
        )

    def group_copy(index):
        h, l, side = index // 4, (index // 2) % 2, index % 2
        return (
            group_out.at[h, l, side], group_in.at[h, y], group_s.at[index], group_r.at[h],
            (x, side, z, 2 * c + l),
        )

    def group_partials(h):
        for l in range(2):
            arrived(local_rows.at[l, pl.ds(6 * h, 6)], local_r.at[2 * h + l])
            if h == 0:
                local_weights[l] = interleave(local_model[l])
            view = local_rows.reshape(2, 12, 256, 128)
            for side in range(2):
                for t3 in range(3):
                    group_out[h, l, side, 128 * t3:128 * t3 + 128, :] = lax.dot_general(
                        view[l, 3 * (2 * h + side) + t3], local_weights[l],
                        (((0,), (0,)), ((), ())), preferred_element_type=F32,
                    ).astype(BF16)

    def send_line(step):
        place = z % 8
        upper = place // 4
        reach = upper * (7 - place) + (1 - upper) * place
        same = 1 - (pair + c) % 2
        for k in range(8):
            n = k + same * (7 - 2 * k)
            inside = (2 * reach - n + 8) // 8
            both = ((n + 1) // 2) * (2 * (n % 2) - 1)
            one = (n - reach) * (1 - 2 * upper)
            s = place + inside * both + (1 - inside) * one
            send(*z_copy(step, s), may_be_me=k == 7)

    def transpose(rows, cols, t):
        cols[128 * t:128 * t + 128, :] = rows.reshape(6, 1024, 128)[t].T

    def expand(rows, step, block):
        start = 256 * block if isinstance(block, int) else pl.multiple_of(256 * block, 256)
        view = rows.reshape(6, 1024, 128)
        lhs = jnp.concatenate([view[t, pl.ds(start, 256), :] for t in range(6)], 1)
        rhs = inbox[step].reshape(768, 128)
        product[...] = jnp.dot(lhs, rhs, preferred_element_type=F32)
        real = product[pl.ds(0, 128, stride=2), :]
        imag = product[pl.ds(1, 128, stride=2), :]
        return real - pltpu.roll(imag, 64, 1) * sign

    def exchange(step, block, slot):
        return remote(
            own_sum.at[step, block], sib_sum.at[step, slot], ex_s.at[step, slot],
            ex_r.at[step, slot], sibling,
        )

    def receive_line(step):
        for s in range(8):
            arrived(inbox.at[step, s], z_r.at[step, s])

    def residual(step):
        receive_line(step)
        for block in range(4):
            part = expand(left_rows, step, block)
            kept = jnp.where(block // 2 == c, recorded_half[block % 2], 0.0)
            own_sum[step, block] = part - kept
            exchange(step, block, block).start()
        for block in range(4):
            exchange(step, block, block).wait_recv()
            values = own_sum[step, block] + sib_sum[step, block]
            if step == 2:
                misfit_full[block] = values
            set_weights(block, values)

    def update(step):
        receive_line(step)
        for q in range(2):
            block = 2 * (1 - c) + q
            own_sum[step, block] = expand(right_rows, step, block)
            exchange(step, block, q).start()
        for q in range(2):
            own_sum[step, 2 * c + q] = expand(right_rows, step, 2 * c + q)
        for q in range(2):
            exchange(step, 2 * (1 - c) + q, q).wait_recv()
            total = own_sum[step, 2 * c + q] + sib_sum[step, q]
            model_half[q] = model_half[q] - STEP_SIZE * total

    SPREAD = [(dx, dc, q) for dx in (2, 1, 3, 0) for dc in (1, 0) for q in range(2)]

    def spread_copy(outer, index):
        dx, dc, q = SPREAD[index]
        column, core = (x + dx) % 4, (c + dc) % 2
        return (
            spread_out.at[outer, q, pl.ds(pl.multiple_of(32 * column + 16 * core, 16), 16)],
            spread_in.at[outer, 4 * x + y],
            sp_s.at[outer, index], sp_r.at[outer],
            (column, core, z, 2 * c + q),
        )

    def sparsify(outer):
        spread_out[outer] = model_half[...].astype(BF16)

        for index in range(16):
            send(*spread_copy(outer, index), may_be_me=index >= 14)
        arrived(spread_in.at[outer], sp_r.at[outer])
        spread_f32[...] = spread_in[outer].reshape(256, 128).astype(F32)
        flat = traces.reshape(256, 128)
        sample = lax.broadcasted_iota(jnp.int32, (NT, 128), 0).astype(F32)
        for p in range(8):
            even = spread_f32[pl.ds(2 * p, 16, stride=16), :]
            odd = spread_f32[pl.ds(2 * p + 1, 16, stride=16), :]
            real = jnp.where(low, even, pltpu.roll(odd, 64, 1))
            imag = jnp.where(low, pltpu.roll(even, 64, 1), odd)
            both = jnp.concatenate([real, imag], 0).astype(BF16)
            series = jnp.dot(
                wave[...], jnp.concatenate([both, both, both], 0), preferred_element_type=F32
            ) * (1.0 / math.sqrt(NF))
            series = jnp.where(sample >= window[p:p + 1, :], series, 0.0)
            series = series - jnp.clip(series, -cutoff, cutoff)
            high = series.astype(BF16)
            rest = (series - high.astype(F32)).astype(BF16)
            first = jnp.dot(wave_back[...], high, preferred_element_type=F32)
            second = jnp.dot(wave_back[0:32, :], rest, preferred_element_type=F32)
            returned = (first[0:32] + first[32:64] + second) * (2.0 * math.sqrt(NF) / NT)
            real, imag = returned[0:16], returned[16:32]
            flat[pl.ds(2 * p, 16, stride=16), :] = jnp.where(low, real, pltpu.roll(imag, 64, 1))
            flat[pl.ds(2 * p + 1, 16, stride=16), :] = jnp.where(low, pltpu.roll(real, 64, 1), imag)

    BACK = [(dx, dy, dc) for dx, dy in PLANE for dc in (1, 0)]

    def back_copy(index):
        dx, dy, dc = BACK[index]
        column, row, core = (x + dx) % 4, (y + dy) % 4, (c + dc) % 2
        return (
            traces_b.at[4 * column + row],
            model_full.at[pl.ds(pl.multiple_of(128 * y + 32 * x + 16 * c, 16), 16)],
            back_s.at[index], back_r.at[0],
            (column, core, z, row),
        )

    def final_copy(index):
        return (
            traces.at[pl.ds(2 * index, 2)],
            estimate_out.at[:, pl.ds(pl.multiple_of(32 * x + 16 * c, 16), 16)],
            fin_s.at[index], fin_r.at[0],
            (index // 2, index % 2, z, y),
        )

    def misfit_copy(q):
        return (
            misfit_full.at[2 * c + q], misfit_out.at[y % 2], mis_s.at[q], mis_r.at[0],
            (x, y // 2, z, 2 * c + q),
        )

    local_model_copy.wait()
    group_partials(0)
    pl.semaphore_wait(barrier, 39 - (pair == c).astype(jnp.int32))
    for index in range(4):
        send(*group_copy(index))
    group_partials(1)
    for index in range(4, 8):
        send(*group_copy(index))
    for t in range(2):
        send_basis(1, t)
    for h in range(2):
        arrived(group_in.at[h], group_r.at[h])
        total = group_in[h, 0].astype(F32)
        for g in range(1, 4):
            total = total + group_in[h, g].astype(F32)
        fill_outbox(0, h, total)
        for t in range(2 * h + 2, 2 * h + 4):
            send_basis(1, t)
    for l in range(2):
        send(*init_copies(l)[1])
    for copy in small:
        copy.wait()

    mute_t = mute[...].astype(F32).T
    mute_rows[...] = jnp.concatenate([mute_t, mute_t], 1)
    first_row = pl.multiple_of(32 * x + 16 * c, 16)
    window = jnp.where(
        low, mute_rows[pl.ds(first_row, 8, stride=2), :], mute_rows[pl.ds(first_row + 1, 8, stride=2), :]
    )
    cutoff = jnp.concatenate([thresholds[...], thresholds[...]], 1)

    for t in range(6):
        arrived(left_rows.at[t], basis_r.at[1, t])
        send_basis(0, t)
        transpose(left_rows, left_cols, t)
    for l in range(2):
        send(*init_copies(l)[0])
    arrived(recorded_half, init_r.at[1])

    for outer in range(2):
        if outer == 1:
            partials(2, right_cols, 0)
            partials(2, right_cols, 1)
            send_line(2)
        residual(2 * outer)
        partials(2 * outer + 1, left_cols, 0)
        partials(2 * outer + 1, left_cols, 1)
        send_line(2 * outer + 1)
        if outer == 1:
            for q in range(2):
                send(*misfit_copy(q))
        else:
            for t in range(6):
                arrived(right_rows.at[t], basis_r.at[0, t])
                transpose(right_rows, right_cols, t)
            arrived(model_half, init_r.at[0])
        update(2 * outer + 1)
        sparsify(outer)
        if outer == 0:
            traces_b[...] = traces[...].astype(BF16)

            for index in range(32):
                send(*back_copy(index), may_be_me=index == 31)
            arrived(model_full, back_r.at[0])
            for block in range(4):
                set_weights(block, model_full[128 * block:128 * block + 128, :].astype(F32))
            for q in range(2):
                rows = pl.ds(pl.multiple_of(256 * c + 128 * q, 128), 128)
                model_half[q] = model_full[rows, :].astype(F32)

    def final_one(index, carry):
        send(*final_copy(index))
        return carry
    lax.fori_loop(0, 8, final_one, 0)

    def basis_done(index, carry):
        for which in range(2):
            sent(*basis_copy(which, index // 4, index % 4))
        return carry
    lax.fori_loop(0, 24, basis_done, 0)
    for l in range(2):
        for item in init_copies(l):
            sent(*item)
        sent(*misfit_copy(l))
    for index in range(8):
        sent(*group_copy(index))
    for step in range(4):
        def z_done(s, carry):
            sent(*z_copy(step, s))
            return carry
        lax.fori_loop(0, 8, z_done, 0)
        if step % 2 == 0:
            for block in range(4):
                exchange(step, block, block).wait_send()
        else:
            for q in range(2):
                exchange(step, 2 * (1 - c) + q, q).wait_send()

    for index in range(16):
        for outer in range(2):
            sent(*spread_copy(outer, index), may_be_me=index >= 14)
    for index in range(32):
        sent(*back_copy(index), may_be_me=index == 31)

    def final_done(index, carry):
        sent(*final_copy(index))
        return carry
    lax.fori_loop(0, 8, final_done, 0)
    arrived(misfit_out, mis_r.at[0])
    arrived(estimate_out, fin_r.at[0])


def body(left_basis, right_basis, start_model, recorded, tile_ranks, mute_start, thresholds):
    def lanes(basis):
        return basis.reshape(2, 128, 2, 12, 128).transpose(0, 1, 3, 2, 4)

    wave, wave_back = wave_tables()
    anywhere = pl.BlockSpec(memory_space=pl.ANY)
    dma = pltpu.SemaphoreType.DMA
    field = jax.ShapeDtypeStruct((2, 128, 128), F32)
    return pl.pallas_call(
        kernel,
        out_shape=(field, field),
        in_specs=[anywhere] * 4 + [pl.BlockSpec(memory_space=pltpu.SMEM)] + [anywhere] * 4,
        out_specs=(anywhere, anywhere),
        scratch_shapes=[
            pltpu.VMEM((6, 512, 2, 128), BF16),
            pltpu.VMEM((6, 512, 2, 128), BF16),
            pltpu.VMEM((768, 1024), BF16),
            pltpu.VMEM((768, 1024), BF16),
            pltpu.VMEM((512, 128), BF16),
            pltpu.VMEM((2, 128, 128), F32),
            pltpu.VMEM((2, 128, 128), F32),
            pltpu.VMEM((256, 128), F32),
            pltpu.VMEM((1024, 128), BF16),
            pltpu.VMEM((256, 128), F32),
            pltpu.VMEM((4, 8, 96, 128), BF16),
            pltpu.VMEM((4, 8, 96, 128), BF16),
            pltpu.VMEM((4, 4, 128, 128), F32),
            pltpu.VMEM((4, 4, 128, 128), F32),
            pltpu.VMEM((4, 128, 128), F32),
            pltpu.VMEM((2, 2, 128, 128), BF16),
            pltpu.VMEM((2, 16, 16, 128), BF16),
            pltpu.VMEM((256, 128), F32),
            pltpu.VMEM((16, 16, 128), F32),
            pltpu.VMEM((16, 16, 128), BF16),
            pltpu.VMEM((128, 128), F32),
            pltpu.VMEM((64, 128), jnp.int32),
            pltpu.VMEM((1, 64), F32),
            pltpu.VMEM((NT, 96), BF16),
            pltpu.VMEM((64, NT), BF16),
            dma((4,)),
            pltpu.VMEM((2, 12, 128, 2, 128), BF16),
            pltpu.VMEM((2, 128, 128), F32),
            pltpu.VMEM((2, 256, 128), BF16),
            pltpu.VMEM((2, 2, 2, 384, 128), BF16),
            pltpu.VMEM((2, 4, 384, 128), BF16),
            dma((5,)), dma((8,)), dma((2,)),
            dma((2, 24)), dma((2, 6)), dma((4,)), dma((2,)),
            dma((4, 8)), dma((4, 8)), dma((4, 4)), dma((4, 4)),
            dma((2, 16)), dma((2,)), dma((32,)), dma((1,)), dma((8,)), dma((1,)), dma((2,)), dma((1,)),
        ],
        compiler_params=pltpu.CompilerParams(
            collective_id=0, has_side_effects=True, vmem_limit_bytes=60 * 1024 * 1024
        ),
    )(
        lanes(left_basis), lanes(right_basis), start_model, recorded, tile_ranks,
        mute_start.T, thresholds.reshape(1, 64), jnp.asarray(wave), jnp.asarray(wave_back),
    )


def solution(mesh):
    return jax.shard_map(
        body,
        mesh=mesh,
        in_specs=(
            P("freq", "tile", None, None),
            P("freq", "tile", None, None),
            P("freq", "tile", None),
            P("freq", "tile", None),
            P(),
            P("tile", None),
            P(),
        ),
        out_specs=(P("freq", "tile", None), P("freq", "tile", None)),
        check_vma=False,
    )
```

```python
import math

import jax
import jax.numpy as jnp
import ml_dtypes
import numpy as np
from jax import lax
from jax.experimental import pallas as pl
from jax.experimental.pallas import tpu as pltpu
from jax.sharding import PartitionSpec as P

F32 = jnp.float32
BF16 = jnp.bfloat16
NT = 256
NF = 16
STEP_SIZE = 0.5
PLANE = sorted(
    ((dx, dy) for dx in range(4) for dy in range(4)),
    key=lambda o: (-min(o[0], 4 - o[0]) - min(o[1], 4 - o[1]), o),
)


def split_table(table, terms):
    parts = []
    rest = table
    for _ in range(terms):
        part = rest.astype(ml_dtypes.bfloat16)
        parts.append(part)
        rest = rest - part.astype(np.float64)
    return parts


def wave_tables():
    sample = np.arange(NT)[:, None]
    bins = np.arange(NF)[None, :] + NT // 4
    phases = (sample * bins % NT) * (2.0 * math.pi / NT)
    table = np.concatenate([np.cos(phases), -np.sin(phases)], 1)
    forward = np.concatenate(split_table(table, 3), 1)
    backward = np.concatenate(split_table(np.ascontiguousarray(table.T), 2), 0)
    return forward, backward


def kernel(
    left, right, model0, recorded, ranks, mute_in, thresholds_in, wave_in, wave_back_in,
    estimate_out, misfit_out,
    left_rows, right_rows, left_cols, right_cols,
    model_full, model_half, recorded_half, packed, weights, product,
    outbox, inbox, own_sum, sib_sum, misfit_full,
    spread_out, spread_in, spread_f32, traces, traces_b, mute_rows, window_rows,
    mute, thresholds, wave, wave_back, small_s,
    local_rows, local_model, local_weights, group_out, group_in, local_r, group_s, group_r, heard,
    basis_s, basis_r, init_s, init_r, z_s, z_r, ex_s, ex_r,
    sp_s, sp_r, back_s, back_r, fin_s, fin_r, mis_s, mis_r,
):
    freq_id = lax.axis_index("freq")
    tile_id = lax.axis_index("tile")
    x, c = freq_id // 2, freq_id % 2
    z, y = tile_id // 4, tile_id % 4
    pair = z // 8
    me = (x, c, z, y)

    def address(place):
        return (place[0] * 2 + place[1], place[2] * 4 + place[3])

    def is_me(place):
        to = address(place)
        return jnp.logical_and(to[0] == freq_id, to[1] == tile_id)

    def remote(src, dst, send_sem, recv_sem, place):
        return pltpu.make_async_remote_copy(
            src_ref=src, dst_ref=dst, send_sem=send_sem, recv_sem=recv_sem,
            device_id=address(place), device_id_type=pl.DeviceIdType.MESH,
        )

    def send(src, dst, send_sem, recv_sem, place, may_be_me=True):
        if not may_be_me:
            remote(src, dst, send_sem, recv_sem, place).start()
            return
        mine = is_me(place)

        @pl.when(jnp.logical_not(mine))
        def _():
            remote(src, dst, send_sem, recv_sem, place).start()

        @pl.when(mine)
        def _():
            pltpu.make_async_copy(src, dst, recv_sem).start()

    def sent(src, dst, send_sem, recv_sem, place, may_be_me=True):
        if not may_be_me:
            remote(src, dst, send_sem, recv_sem, place).wait_send()
            return

        @pl.when(jnp.logical_not(is_me(place)))
        def _():
            remote(src, dst, send_sem, recv_sem, place).wait_send()

    def arrived(ref, sem):
        pltpu.make_async_copy(ref, ref, sem).wait()

    barrier = pltpu.get_barrier_semaphore()

    def greet(place):
        pl.semaphore_signal(
            barrier, inc=1, device_id=address(place), device_id_type=pl.DeviceIdType.MESH
        )

    small = [
        pltpu.make_async_copy(src, dst, small_s.at[i])
        for i, (src, dst) in enumerate(
            ((mute_in, mute), (thresholds_in, thresholds), (wave_in, wave), (wave_back_in, wave_back))
        )
    ]

    local_model_copy = pltpu.make_async_copy(model0, local_model, local_r.at[4])
    local_model_copy.start()

    def local_load(h):
        for l in range(2):
            for side in range(2):
                for t3 in range(3):
                    t = 6 * side + 3 * h + t3
                    pltpu.make_async_copy(
                        right.at[l, :, t], local_rows.at[l, 3 * (2 * h + side) + t3], local_r.at[2 * h + l]
                    ).start()

    local_load(0)
    local_load(1)
    for dx, dz, dy in ((0, 0, 2), (0, 1, 0), (0, 15, 0), (1, 0, 0), (3, 0, 0), (0, 0, 1), (0, 0, 3), (0, 0, 0)):
        for dc in (1, 0):
            if (dx, dz, dy, dc) != (0, 0, 0, 0):
                greet(((x + dx) % 4, (c + dc) % 2, (z + dz) % 16, (y + dy) % 4))

    def tell(index, steps):
        for dx, dz in steps:
            pl.semaphore_signal(
                heard.at[index], inc=1, device_id=address(((x + dx) % 4, c, (z + dz) % 16, y)),
                device_id_type=pl.DeviceIdType.MESH,
            )

    def hear(index):
        pl.semaphore_wait(heard.at[index], 2)

    for copy in small:
        copy.start()

    def basis_copy(which, t, q):
        source = (right, left)[which]
        rows = (right_rows, left_rows)[which]
        side, l = q // 2, q % 2
        return (
            source.at[l, :, 6 * side + t],
            rows.at[t, pl.ds(128 * y, 128)],
            basis_s.at[which, 4 * t + q],
            basis_r.at[which, t],
            (x, side, z, 2 * c + l),
        )

    def send_basis(which, t):
        def one(q, carry):
            send(*basis_copy(which, t, q))
            return carry
        lax.fori_loop(0, 4, one, 0)

    def init_copies(l):
        place = (x, y // 2, z, 2 * c + l)
        return (
            (model0.at[l], model_half.at[y % 2], init_s.at[l], init_r.at[0], place),
            (recorded.at[l], recorded_half.at[y % 2], init_s.at[2 + l], init_r.at[1], place),
        )

    sibling = (x, 1 - c, z, y)
    lane = lax.broadcasted_iota(jnp.int32, (1, 128), 1)
    low = lane < 64
    sign = jnp.where(low, 1.0, -1.0).astype(F32)

    def interleave(values):
        values = values.astype(BF16).astype(F32)
        packed[pl.ds(0, 128, stride=2), :] = values
        packed[pl.ds(1, 128, stride=2), :] = pltpu.roll(values, 64, 1) * sign
        return packed[...].astype(BF16)

    def set_weights(block, values):
        weights[256 * block:256 * block + 256, :] = interleave(values)

    slots = lax.broadcasted_iota(jnp.int32, (96, 128), 0)

    def z_copy(step, s):
        return (
            outbox.at[step, s], inbox.at[step, z % 8], z_s.at[step, s], z_r.at[step, z % 8],
            (x, pair, 8 * c + s, y),
        )

    def fill_outbox(step, h, values):
        for s4 in range(4):
            s = 4 * h + s4
            other = 8 * c + s
            rank = ranks[other, z] if step % 2 == 0 else ranks[z, other]
            part = values[96 * s4:96 * s4 + 96, :]
            outbox[step, s] = jnp.where(slots < rank, part, 0.0).astype(BF16)
            if step == 0:
                send(*z_copy(step, s))

    def partials(step, cols, h):
        fill_outbox(
            step, h,
            jnp.dot(cols[384 * h:384 * h + 384, :], weights[...], preferred_element_type=F32),
        )

    def group_copy(index):
        h, l, side = index // 4, (index // 2) % 2, index % 2
        return (
            group_out.at[h, l, side], group_in.at[h, y], group_s.at[index], group_r.at[h],
            (x, side, z, 2 * c + l),
        )

    def group_partials(h):
        for l in range(2):
            arrived(local_rows.at[l, pl.ds(6 * h, 6)], local_r.at[2 * h + l])
            if h == 0:
                local_weights[l] = interleave(local_model[l])
            view = local_rows.reshape(2, 12, 256, 128)
            def one_block(index, carry):
                rows = pl.ds(pl.multiple_of(128 * (index % 3), 128), 128)
                group_out[h, l, index // 3, rows, :] = lax.dot_general(
                    view[l, 6 * h + index], local_weights[l],
                    (((0,), (0,)), ((), ())), preferred_element_type=F32,
                ).astype(BF16)
                return carry
            lax.fori_loop(0, 6, one_block, 0)

    def send_line(step):
        place = z % 8
        upper = place // 4
        reach = upper * (7 - place) + (1 - upper) * place
        same = 1 - (pair + c) % 2
        for k in range(8):
            n = k + same * (7 - 2 * k)
            inside = (2 * reach - n + 8) // 8
            both = ((n + 1) // 2) * (2 * (n % 2) - 1)
            one = (n - reach) * (1 - 2 * upper)
            s = place + inside * both + (1 - inside) * one
            send(*z_copy(step, s), may_be_me=k == 7)

    def transpose(rows, cols, t):
        cols[pl.ds(pl.multiple_of(128 * t, 128), 128), :] = rows.reshape(6, 1024, 128)[t].T

    def expand(rows, step, block):
        start = 256 * block if isinstance(block, int) else pl.multiple_of(256 * block, 256)
        view = rows.reshape(6, 1024, 128)
        lhs = jnp.concatenate([view[t, pl.ds(start, 256), :] for t in range(6)], 1)
        rhs = inbox[step].reshape(768, 128)
        product[...] = jnp.dot(lhs, rhs, preferred_element_type=F32)
        real = product[pl.ds(0, 128, stride=2), :]
        imag = product[pl.ds(1, 128, stride=2), :]
        return real - pltpu.roll(imag, 64, 1) * sign

    def exchange(step, block, slot):
        return remote(
            own_sum.at[step, block], sib_sum.at[step, slot], ex_s.at[step, slot],
            ex_r.at[step, slot], sibling,
        )

    def receive_line(step):
        for s in range(8):
            arrived(inbox.at[step, s], z_r.at[step, s])

    def residual(step):
        receive_line(step)
        def one_sum(block, carry):
            part = expand(left_rows, step, block)
            kept = jnp.where(block // 2 == c, recorded_half[block % 2], 0.0)
            own_sum[step, block] = part - kept
            exchange(step, block, block).start()
            return carry
        lax.fori_loop(0, 4, one_sum, 0)
        for block in range(4):
            exchange(step, block, block).wait_recv()
            values = own_sum[step, block] + sib_sum[step, block]
            if step == 2:
                misfit_full[block] = values
            set_weights(block, values)

    def update(step):
        receive_line(step)
        def one_sum(index, carry):
            block = (2 * (1 - c) + index) % 4
            own_sum[step, block] = expand(right_rows, step, block)

            @pl.when(index < 2)
            def _():
                exchange(step, block, index % 2).start()
            return carry
        lax.fori_loop(0, 4, one_sum, 0)
        if step == 1:
            arrived(model_half, init_r.at[0])
        for q in range(2):
            exchange(step, 2 * (1 - c) + q, q).wait_recv()
            total = own_sum[step, 2 * c + q] + sib_sum[step, q]
            model_half[q] = model_half[q] - STEP_SIZE * total

    SPREAD = [(dx, dc, q) for dx in (2, 1, 3, 0) for dc in (1, 0) for q in range(2)]

    def spread_copy(outer, index):
        dx, dc, q = SPREAD[index]
        column, core = (x + dx) % 4, (c + dc) % 2
        return (
            spread_out.at[outer, q, pl.ds(pl.multiple_of(32 * column + 16 * core, 16), 16)],
            spread_in.at[outer, 4 * x + y],
            sp_s.at[outer, index], sp_r.at[outer],
            (column, core, z, 2 * c + q),
        )

    def sparsify(outer):
        spread_out[outer] = model_half[...].astype(BF16)

        for index in range(16):
            send(*spread_copy(outer, index), may_be_me=index >= 14)
        arrived(spread_in.at[outer], sp_r.at[outer])
        spread_f32[...] = spread_in[outer].reshape(256, 128).astype(F32)
        flat = traces.reshape(256, 128)
        sample = lax.broadcasted_iota(jnp.int32, (NT, 128), 0).astype(F32)

        def one_pair(p, carry):
            even = spread_f32[pl.ds(2 * p, 16, stride=16), :]
            odd = spread_f32[pl.ds(2 * p + 1, 16, stride=16), :]
            real = jnp.where(low, even, pltpu.roll(odd, 64, 1))
            imag = jnp.where(low, pltpu.roll(even, 64, 1), odd)
            both = jnp.concatenate([real, imag], 0).astype(BF16)
            series = jnp.dot(
                wave[...], jnp.concatenate([both, both, both], 0), preferred_element_type=F32
            ) * (1.0 / math.sqrt(NF))
            series = jnp.where(sample >= window_rows[pl.ds(p, 1), :], series, 0.0)
            series = series - jnp.clip(series, -cutoff, cutoff)
            high = series.astype(BF16)
            rest = (series - high.astype(F32)).astype(BF16)
            first = jnp.dot(wave_back[...], high, preferred_element_type=F32)
            second = jnp.dot(wave_back[0:32, :], rest, preferred_element_type=F32)
            returned = (first[0:32] + first[32:64] + second) * (2.0 * math.sqrt(NF) / NT)
            real, imag = returned[0:16], returned[16:32]
            flat[pl.ds(2 * p, 16, stride=16), :] = jnp.where(low, real, pltpu.roll(imag, 64, 1))
            flat[pl.ds(2 * p + 1, 16, stride=16), :] = jnp.where(low, pltpu.roll(real, 64, 1), imag)
            return carry
        lax.fori_loop(0, 8, one_pair, 0)

    BACK = [(dx, dy, dc) for dx, dy in PLANE for dc in (1, 0)]

    def back_copy(index):
        dx, dy, dc = BACK[index]
        column, row, core = (x + dx) % 4, (y + dy) % 4, (c + dc) % 2
        return (
            traces_b.at[4 * column + row],
            model_full.at[pl.ds(pl.multiple_of(128 * y + 32 * x + 16 * c, 16), 16)],
            back_s.at[index], back_r.at[0],
            (column, core, z, row),
        )

    def final_copy(index):
        return (
            traces.at[pl.ds(2 * index, 2)],
            estimate_out.at[:, pl.ds(pl.multiple_of(32 * x + 16 * c, 16), 16)],
            fin_s.at[index], fin_r.at[0],
            (index // 2, index % 2, z, y),
        )

    def misfit_copy(q):
        return (
            misfit_full.at[2 * c + q], misfit_out.at[y % 2], mis_s.at[q], mis_r.at[0],
            (x, y // 2, z, 2 * c + q),
        )

    local_model_copy.wait()
    group_partials(0)
    pl.semaphore_wait(barrier, 15)
    for index in range(4):
        send(*group_copy(index))
    tell(0, ((0, 1), (0, 15)))
    tell(3, ((1, 0), (3, 0)))
    group_partials(1)
    for index in range(4, 8):
        send(*group_copy(index))
    for t in range(2):
        send_basis(1, t)
    hear(0)
    tell(1, ((0, 2), (0, 14)))
    hear(1)
    tell(2, ((0, 4), (0, 12)))
    hear(3)
    tell(4, ((1, 0), (3, 0)))
    hear(2)
    hear(4)
    for h in range(2):
        arrived(group_in.at[h], group_r.at[h])
        total = group_in[h, 0].astype(F32)
        for g in range(1, 4):
            total = total + group_in[h, g].astype(F32)
        fill_outbox(0, h, total)
        for t in range(2 * h + 2, 2 * h + 4):
            send_basis(1, t)
    for l in range(2):
        send(*init_copies(l)[1])
    for copy in small:
        copy.wait()

    mute_t = mute[...].astype(F32).T
    mute_rows[...] = jnp.concatenate([mute_t, mute_t], 1)
    first_row = pl.multiple_of(32 * x + 16 * c, 16)
    window_rows[...] = jnp.where(
        low, mute_rows[pl.ds(first_row, 8, stride=2), :], mute_rows[pl.ds(first_row + 1, 8, stride=2), :]
    )
    cutoff = jnp.concatenate([thresholds[...], thresholds[...]], 1)

    def left_block(t, carry):
        arrived(left_rows.at[t], basis_r.at[1, t])
        send_basis(0, t)
        transpose(left_rows, left_cols, t)
        return carry
    lax.fori_loop(0, 6, left_block, 0)
    for l in range(2):
        send(*init_copies(l)[0])
    arrived(recorded_half, init_r.at[1])

    for outer in range(2):
        if outer == 1:
            partials(2, right_cols, 0)
            partials(2, right_cols, 1)
            send_line(2)
        residual(2 * outer)
        partials(2 * outer + 1, left_cols, 0)
        partials(2 * outer + 1, left_cols, 1)
        send_line(2 * outer + 1)
        if outer == 1:
            for q in range(2):
                send(*misfit_copy(q))
        else:
            def right_block(t, carry):
                arrived(right_rows.at[t], basis_r.at[0, t])
                transpose(right_rows, right_cols, t)
                return carry
            lax.fori_loop(0, 6, right_block, 0)
        update(2 * outer + 1)
        sparsify(outer)
        if outer == 0:
            traces_b[...] = traces[...].astype(BF16)

            for index in range(32):
                send(*back_copy(index), may_be_me=index == 31)
            arrived(model_full, back_r.at[0])
            for block in range(4):
                set_weights(block, model_full[128 * block:128 * block + 128, :].astype(F32))
            for q in range(2):
                rows = pl.ds(pl.multiple_of(256 * c + 128 * q, 128), 128)
                model_half[q] = model_full[rows, :].astype(F32)

    def final_one(index, carry):
        send(*final_copy(index))
        return carry
    lax.fori_loop(0, 8, final_one, 0)

    def basis_done(index, carry):
        for which in range(2):
            sent(*basis_copy(which, index // 4, index % 4))
        return carry
    lax.fori_loop(0, 24, basis_done, 0)
    for l in range(2):
        for item in init_copies(l):
            sent(*item)
        sent(*misfit_copy(l))
    for index in range(8):
        sent(*group_copy(index))
    for step in range(4):
        def z_done(s, carry):
            sent(*z_copy(step, s))
            return carry
        lax.fori_loop(0, 8, z_done, 0)
        if step % 2 == 0:
            for block in range(4):
                exchange(step, block, block).wait_send()
        else:
            for q in range(2):
                exchange(step, 2 * (1 - c) + q, q).wait_send()

    for index in range(16):
        for outer in range(2):
            sent(*spread_copy(outer, index), may_be_me=index >= 14)
    for index in range(32):
        sent(*back_copy(index), may_be_me=index == 31)

    def final_done(index, carry):
        sent(*final_copy(index))
        return carry
    lax.fori_loop(0, 8, final_done, 0)
    arrived(misfit_out, mis_r.at[0])
    arrived(estimate_out, fin_r.at[0])


def body(left_basis, right_basis, start_model, recorded, tile_ranks, mute_start, thresholds):
    def lanes(basis):
        return basis.reshape(2, 128, 2, 12, 128).transpose(0, 1, 3, 2, 4)

    wave, wave_back = wave_tables()
    anywhere = pl.BlockSpec(memory_space=pl.ANY)
    dma = pltpu.SemaphoreType.DMA
    field = jax.ShapeDtypeStruct((2, 128, 128), F32)
    return pl.pallas_call(
        kernel,
        out_shape=(field, field),
        in_specs=[anywhere] * 4 + [pl.BlockSpec(memory_space=pltpu.SMEM)] + [anywhere] * 4,
        out_specs=(anywhere, anywhere),
        scratch_shapes=[
            pltpu.VMEM((6, 512, 2, 128), BF16),
            pltpu.VMEM((6, 512, 2, 128), BF16),
            pltpu.VMEM((768, 1024), BF16),
            pltpu.VMEM((768, 1024), BF16),
            pltpu.VMEM((512, 128), BF16),
            pltpu.VMEM((2, 128, 128), F32),
            pltpu.VMEM((2, 128, 128), F32),
            pltpu.VMEM((256, 128), F32),
            pltpu.VMEM((1024, 128), BF16),
            pltpu.VMEM((256, 128), F32),
            pltpu.VMEM((4, 8, 96, 128), BF16),
            pltpu.VMEM((4, 8, 96, 128), BF16),
            pltpu.VMEM((4, 4, 128, 128), F32),
            pltpu.VMEM((4, 4, 128, 128), F32),
            pltpu.VMEM((4, 128, 128), F32),
            pltpu.VMEM((2, 2, 128, 128), BF16),
            pltpu.VMEM((2, 16, 16, 128), BF16),
            pltpu.VMEM((256, 128), F32),
            pltpu.VMEM((16, 16, 128), F32),
            pltpu.VMEM((16, 16, 128), BF16),
            pltpu.VMEM((128, 128), F32),
            pltpu.VMEM((8, 128), F32),
            pltpu.VMEM((64, 128), jnp.int32),
            pltpu.VMEM((1, 64), F32),
            pltpu.VMEM((NT, 96), BF16),
            pltpu.VMEM((64, NT), BF16),
            dma((4,)),
            pltpu.VMEM((2, 12, 128, 2, 128), BF16),
            pltpu.VMEM((2, 128, 128), F32),
            pltpu.VMEM((2, 256, 128), BF16),
            pltpu.VMEM((2, 2, 2, 384, 128), BF16),
            pltpu.VMEM((2, 4, 384, 128), BF16),
            dma((5,)), dma((8,)), dma((2,)), pltpu.SemaphoreType.REGULAR((5,)),
            dma((2, 24)), dma((2, 6)), dma((4,)), dma((2,)),
            dma((4, 8)), dma((4, 8)), dma((4, 4)), dma((4, 4)),
            dma((2, 16)), dma((2,)), dma((32,)), dma((1,)), dma((8,)), dma((1,)), dma((2,)), dma((1,)),
        ],
        compiler_params=pltpu.CompilerParams(
            collective_id=0, has_side_effects=True, vmem_limit_bytes=60 * 1024 * 1024
        ),
    )(
        lanes(left_basis), lanes(right_basis), start_model, recorded, tile_ranks,
        mute_start.T, thresholds.reshape(1, 64), jnp.asarray(wave), jnp.asarray(wave_back),
    )


def solution(mesh):
    return jax.shard_map(
        body,
        mesh=mesh,
        in_specs=(
            P("freq", "tile", None, None),
            P("freq", "tile", None, None),
            P("freq", "tile", None),
            P("freq", "tile", None),
            P(),
            P("tile", None),
            P(),
        ),
        out_specs=(P("freq", "tile", None), P("freq", "tile", None)),
        check_vma=False,
    )
```

```python
import math

import jax
import jax.numpy as jnp
import ml_dtypes
import numpy as np
from jax import lax
from jax.experimental import pallas as pl
from jax.experimental.pallas import tpu as pltpu
from jax.sharding import PartitionSpec as P

F32 = jnp.float32
BF16 = jnp.bfloat16
NT = 256
NF = 16
STEP_SIZE = 0.5
PLANE = sorted(
    ((dx, dy) for dx in range(4) for dy in range(4)),
    key=lambda o: (-min(o[0], 4 - o[0]) - min(o[1], 4 - o[1]), o),
)


def split_table(table, terms):
    parts = []
    rest = table
    for _ in range(terms):
        part = rest.astype(ml_dtypes.bfloat16)
        parts.append(part)
        rest = rest - part.astype(np.float64)
    return parts


def wave_tables():
    sample = np.arange(NT)[:, None]
    bins = np.arange(NF)[None, :] + NT // 4
    phases = (sample * bins % NT) * (2.0 * math.pi / NT)
    table = np.concatenate([np.cos(phases), -np.sin(phases)], 1)
    forward = np.concatenate(split_table(table, 3), 1)
    backward = np.concatenate(split_table(np.ascontiguousarray(table.T), 2), 0)
    return forward, backward


def kernel(
    left, right, model0, recorded, ranks, mute_in, thresholds_in, wave_in, wave_back_in,
    estimate_out, misfit_out,
    left_rows, right_rows, left_cols, right_cols,
    model_full, model_half, recorded_half, packed, weights, product,
    outbox, inbox, own_sum, sib_sum, misfit_full,
    spread_out, spread_in, spread_f32, traces, traces_b, mute_rows, window_rows,
    mute, thresholds, wave, wave_back, small_s,
    local_rows, local_model, local_weights, group_out, group_in, local_r, group_s, group_r, heard,
    basis_s, basis_r, init_s, init_r, z_s, z_r, ex_s, ex_r,
    sp_s, sp_r, back_s, back_r, fin_s, fin_r, mis_s, mis_r,
):
    freq_id = lax.axis_index("freq")
    tile_id = lax.axis_index("tile")
    x, c = freq_id // 2, freq_id % 2
    z, y = tile_id // 4, tile_id % 4
    pair = z // 8
    me = (x, c, z, y)

    def address(place):
        return (place[0] * 2 + place[1], place[2] * 4 + place[3])

    def is_me(place):
        to = address(place)
        return jnp.logical_and(to[0] == freq_id, to[1] == tile_id)

    def remote(src, dst, send_sem, recv_sem, place):
        return pltpu.make_async_remote_copy(
            src_ref=src, dst_ref=dst, send_sem=send_sem, recv_sem=recv_sem,
            device_id=address(place), device_id_type=pl.DeviceIdType.MESH,
        )

    def send(src, dst, send_sem, recv_sem, place, may_be_me=True):
        if not may_be_me:
            remote(src, dst, send_sem, recv_sem, place).start()
            return
        mine = is_me(place)

        @pl.when(jnp.logical_not(mine))
        def _():
            remote(src, dst, send_sem, recv_sem, place).start()

        @pl.when(mine)
        def _():
            pltpu.make_async_copy(src, dst, recv_sem).start()

    def sent(src, dst, send_sem, recv_sem, place, may_be_me=True):
        if not may_be_me:
            remote(src, dst, send_sem, recv_sem, place).wait_send()
            return

        @pl.when(jnp.logical_not(is_me(place)))
        def _():
            remote(src, dst, send_sem, recv_sem, place).wait_send()

    def arrived(ref, sem):
        pltpu.make_async_copy(ref, ref, sem).wait()

    barrier = pltpu.get_barrier_semaphore()

    def greet(place):
        pl.semaphore_signal(
            barrier, inc=1, device_id=address(place), device_id_type=pl.DeviceIdType.MESH
        )

    small = [
        pltpu.make_async_copy(src, dst, small_s.at[i])
        for i, (src, dst) in enumerate(
            ((mute_in, mute), (thresholds_in, thresholds), (wave_in, wave), (wave_back_in, wave_back))
        )
    ]

    local_model_copy = pltpu.make_async_copy(model0, local_model, local_r.at[4])
    local_model_copy.start()

    def local_load(h):
        for l in range(2):
            for side in range(2):
                for t3 in range(3):
                    t = 6 * side + 3 * h + t3
                    pltpu.make_async_copy(
                        right.at[l, :, t], local_rows.at[l, 3 * (2 * h + side) + t3], local_r.at[2 * h + l]
                    ).start()

    local_load(0)
    local_load(1)
    for dx, dz, dy in ((0, 0, 2), (0, 1, 0), (0, 15, 0), (1, 0, 0), (3, 0, 0), (0, 0, 1), (0, 0, 3), (0, 0, 0)):
        for dc in (1, 0):
            if (dx, dz, dy, dc) != (0, 0, 0, 0):
                greet(((x + dx) % 4, (c + dc) % 2, (z + dz) % 16, (y + dy) % 4))

    def tell(index, steps):
        for dx, dz in steps:
            pl.semaphore_signal(
                heard.at[index], inc=1, device_id=address(((x + dx) % 4, c, (z + dz) % 16, y)),
                device_id_type=pl.DeviceIdType.MESH,
            )

    def hear(index):
        pl.semaphore_wait(heard.at[index], 2)

    for copy in small:
        copy.start()

    def basis_copy(which, t, q):
        source = (right, left)[which]
        rows = (right_rows, left_rows)[which]
        side, l = q // 2, q % 2
        return (
            source.at[l, :, 6 * side + t],
            rows.at[t, pl.ds(128 * y, 128)],
            basis_s.at[which, 4 * t + q],
            basis_r.at[which, t],
            (x, side, z, 2 * c + l),
        )

    def send_basis(which, t):
        def one(q, carry):
            send(*basis_copy(which, t, q))
            return carry
        lax.fori_loop(0, 4, one, 0)

    def init_copies(l):
        place = (x, y // 2, z, 2 * c + l)
        return (
            (model0.at[l], model_half.at[y % 2], init_s.at[l], init_r.at[0], place),
            (recorded.at[l], recorded_half.at[y % 2], init_s.at[2 + l], init_r.at[1], place),
        )

    sibling = (x, 1 - c, z, y)
    lane = lax.broadcasted_iota(jnp.int32, (1, 128), 1)
    low = lane < 64
    sign = jnp.where(low, 1.0, -1.0).astype(F32)

    def interleave(values):
        values = values.astype(BF16).astype(F32)
        packed[pl.ds(0, 128, stride=2), :] = values
        packed[pl.ds(1, 128, stride=2), :] = pltpu.roll(values, 64, 1) * sign
        return packed[...].astype(BF16)

    def set_weights(block, values):
        weights[256 * block:256 * block + 256, :] = interleave(values)

    slots = lax.broadcasted_iota(jnp.int32, (96, 128), 0)

    def z_copy(step, s):
        return (
            outbox.at[step, s], inbox.at[step, z % 8], z_s.at[step, s], z_r.at[step, z % 8],
            (x, pair, 8 * c + s, y),
        )

    def fill_outbox(step, h, values):
        for s4 in range(4):
            s = 4 * h + s4
            other = 8 * c + s
            rank = ranks[other, z] if step % 2 == 0 else ranks[z, other]
            part = values[96 * s4:96 * s4 + 96, :]
            outbox[step, s] = jnp.where(slots < rank, part, 0.0).astype(BF16)
            if step == 0:
                send(*z_copy(step, s))

    def partials(step, cols, h):
        fill_outbox(
            step, h,
            jnp.dot(cols[384 * h:384 * h + 384, :], weights[...], preferred_element_type=F32),
        )

    def group_copy(index):
        h, l, side = index // 4, (index // 2) % 2, index % 2
        return (
            group_out.at[h, l, side], group_in.at[h, y], group_s.at[index], group_r.at[h],
            (x, side, z, 2 * c + l),
        )

    def group_partials(h):
        for l in range(2):
            arrived(local_rows.at[l, pl.ds(6 * h, 6)], local_r.at[2 * h + l])
            if h == 0:
                local_weights[l] = interleave(local_model[l])
            view = local_rows.reshape(2, 12, 256, 128)
            def one_block(index, carry):
                rows = pl.ds(pl.multiple_of(128 * (index % 3), 128), 128)
                group_out[h, l, index // 3, rows, :] = lax.dot_general(
                    view[l, 6 * h + index], local_weights[l],
                    (((0,), (0,)), ((), ())), preferred_element_type=F32,
                ).astype(BF16)
                return carry
            for index in range(6):
                one_block(index, 0)

    def send_line(step):
        place = z % 8
        upper = place // 4
        reach = upper * (7 - place) + (1 - upper) * place
        same = 1 - (pair + c) % 2
        for k in range(8):
            n = k + same * (7 - 2 * k)
            inside = (2 * reach - n + 8) // 8
            both = ((n + 1) // 2) * (2 * (n % 2) - 1)
            one = (n - reach) * (1 - 2 * upper)
            s = place + inside * both + (1 - inside) * one
            send(*z_copy(step, s), may_be_me=k == 7)

    def transpose(rows, cols, t):
        cols[pl.ds(pl.multiple_of(128 * t, 128), 128), :] = rows.reshape(6, 1024, 128)[t].T

    def expand(rows, step, block):
        start = 256 * block if isinstance(block, int) else pl.multiple_of(256 * block, 256)
        view = rows.reshape(6, 1024, 128)
        lhs = jnp.concatenate([view[t, pl.ds(start, 256), :] for t in range(6)], 1)
        rhs = inbox[step].reshape(768, 128)
        product[...] = jnp.dot(lhs, rhs, preferred_element_type=F32)
        real = product[pl.ds(0, 128, stride=2), :]
        imag = product[pl.ds(1, 128, stride=2), :]
        return real - pltpu.roll(imag, 64, 1) * sign

    def exchange(step, block, slot):
        return remote(
            own_sum.at[step, block], sib_sum.at[step, slot], ex_s.at[step, slot],
            ex_r.at[step, slot], sibling,
        )

    def receive_line(step):
        for s in range(8):
            arrived(inbox.at[step, s], z_r.at[step, s])

    def residual(step):
        receive_line(step)
        for block in range(4):
            part = expand(left_rows, step, block)
            kept = jnp.where(block // 2 == c, recorded_half[block % 2], 0.0)
            own_sum[step, block] = part - kept
            exchange(step, block, block).start()
        for block in range(4):
            exchange(step, block, block).wait_recv()
            values = own_sum[step, block] + sib_sum[step, block]
            if step == 2:
                misfit_full[block] = values
            set_weights(block, values)

    def update(step):
        receive_line(step)
        for q in range(2):
            block = 2 * (1 - c) + q
            own_sum[step, block] = expand(right_rows, step, block)
            exchange(step, block, q).start()
        for q in range(2):
            own_sum[step, 2 * c + q] = expand(right_rows, step, 2 * c + q)
        if step == 1:
            arrived(model_half, init_r.at[0])
        for q in range(2):
            exchange(step, 2 * (1 - c) + q, q).wait_recv()
            total = own_sum[step, 2 * c + q] + sib_sum[step, q]
            model_half[q] = model_half[q] - STEP_SIZE * total

    SPREAD = [(dx, dc, q) for dx in (2, 1, 3, 0) for dc in (1, 0) for q in range(2)]

    def spread_copy(outer, index):
        dx, dc, q = SPREAD[index]
        column, core = (x + dx) % 4, (c + dc) % 2
        return (
            spread_out.at[outer, q, pl.ds(pl.multiple_of(32 * column + 16 * core, 16), 16)],
            spread_in.at[outer, 4 * x + y],
            sp_s.at[outer, index], sp_r.at[outer],
            (column, core, z, 2 * c + q),
        )

    def sparsify(outer):
        spread_out[outer] = model_half[...].astype(BF16)

        for index in range(16):
            send(*spread_copy(outer, index), may_be_me=index >= 14)
        arrived(spread_in.at[outer], sp_r.at[outer])
        spread_f32[...] = spread_in[outer].reshape(256, 128).astype(F32)
        flat = traces.reshape(256, 128)
        sample = lax.broadcasted_iota(jnp.int32, (NT, 128), 0).astype(F32)

        def one_pair(p, carry):
            even = spread_f32[pl.ds(2 * p, 16, stride=16), :]
            odd = spread_f32[pl.ds(2 * p + 1, 16, stride=16), :]
            real = jnp.where(low, even, pltpu.roll(odd, 64, 1))
            imag = jnp.where(low, pltpu.roll(even, 64, 1), odd)
            both = jnp.concatenate([real, imag], 0).astype(BF16)
            series = jnp.dot(
                wave[...], jnp.concatenate([both, both, both], 0), preferred_element_type=F32
            ) * (1.0 / math.sqrt(NF))
            series = jnp.where(sample >= window_rows[p:p + 1, :], series, 0.0)
            series = series - jnp.clip(series, -cutoff, cutoff)
            high = series.astype(BF16)
            rest = (series - high.astype(F32)).astype(BF16)
            first = jnp.dot(wave_back[...], high, preferred_element_type=F32)
            second = jnp.dot(wave_back[0:32, :], rest, preferred_element_type=F32)
            returned = (first[0:32] + first[32:64] + second) * (2.0 * math.sqrt(NF) / NT)
            real, imag = returned[0:16], returned[16:32]
            flat[pl.ds(2 * p, 16, stride=16), :] = jnp.where(low, real, pltpu.roll(imag, 64, 1))
            flat[pl.ds(2 * p + 1, 16, stride=16), :] = jnp.where(low, pltpu.roll(real, 64, 1), imag)
            return carry
        for p in range(8):
            one_pair(p, 0)

    BACK = [(dx, dy, dc) for dx, dy in PLANE for dc in (1, 0)]

    def back_copy(index):
        dx, dy, dc = BACK[index]
        column, row, core = (x + dx) % 4, (y + dy) % 4, (c + dc) % 2
        return (
            traces_b.at[4 * column + row],
            model_full.at[pl.ds(pl.multiple_of(128 * y + 32 * x + 16 * c, 16), 16)],
            back_s.at[index], back_r.at[0],
            (column, core, z, row),
        )

    def final_copy(index):
        return (
            traces.at[pl.ds(2 * index, 2)],
            estimate_out.at[:, pl.ds(pl.multiple_of(32 * x + 16 * c, 16), 16)],
            fin_s.at[index], fin_r.at[0],
            (index // 2, index % 2, z, y),
        )

    def misfit_copy(q):
        return (
            misfit_full.at[2 * c + q], misfit_out.at[y % 2], mis_s.at[q], mis_r.at[0],
            (x, y // 2, z, 2 * c + q),
        )

    local_model_copy.wait()
    group_partials(0)
    pl.semaphore_wait(barrier, 15)
    for index in range(4):
        send(*group_copy(index))
    tell(0, ((0, 1), (0, 15)))
    tell(3, ((1, 0), (3, 0)))
    group_partials(1)
    for index in range(4, 8):
        send(*group_copy(index))
    for t in range(2):
        send_basis(1, t)
    hear(0)
    tell(1, ((0, 2), (0, 14)))
    hear(1)
    tell(2, ((0, 4), (0, 12)))
    hear(3)
    tell(4, ((1, 0), (3, 0)))
    hear(2)
    hear(4)
    for h in range(2):
        arrived(group_in.at[h], group_r.at[h])
        total = group_in[h, 0].astype(F32)
        for g in range(1, 4):
            total = total + group_in[h, g].astype(F32)
        fill_outbox(0, h, total)
        for t in range(2 * h + 2, 2 * h + 4):
            send_basis(1, t)
    for l in range(2):
        send(*init_copies(l)[1])
    for copy in small:
        copy.wait()

    mute_t = mute[...].astype(F32).T
    mute_rows[...] = jnp.concatenate([mute_t, mute_t], 1)
    first_row = pl.multiple_of(32 * x + 16 * c, 16)
    window_rows[...] = jnp.where(
        low, mute_rows[pl.ds(first_row, 8, stride=2), :], mute_rows[pl.ds(first_row + 1, 8, stride=2), :]
    )
    cutoff = jnp.concatenate([thresholds[...], thresholds[...]], 1)

    def left_block(t, carry):
        arrived(left_rows.at[t], basis_r.at[1, t])
        send_basis(0, t)
        transpose(left_rows, left_cols, t)
        return carry
    lax.fori_loop(0, 6, left_block, 0)
    for l in range(2):
        send(*init_copies(l)[0])
    arrived(recorded_half, init_r.at[1])

    for outer in range(2):
        if outer == 1:
            partials(2, right_cols, 0)
            partials(2, right_cols, 1)
            send_line(2)
        residual(2 * outer)
        partials(2 * outer + 1, left_cols, 0)
        partials(2 * outer + 1, left_cols, 1)
        send_line(2 * outer + 1)
        if outer == 1:
            for q in range(2):
                send(*misfit_copy(q))
        else:
            def right_block(t, carry):
                arrived(right_rows.at[t], basis_r.at[0, t])
                transpose(right_rows, right_cols, t)
                return carry
            lax.fori_loop(0, 6, right_block, 0)
        update(2 * outer + 1)
        sparsify(outer)
        if outer == 0:
            traces_b[...] = traces[...].astype(BF16)

            for index in range(32):
                send(*back_copy(index), may_be_me=index == 31)
            arrived(model_full, back_r.at[0])
            for block in range(4):
                set_weights(block, model_full[128 * block:128 * block + 128, :].astype(F32))
            for q in range(2):
                rows = pl.ds(pl.multiple_of(256 * c + 128 * q, 128), 128)
                model_half[q] = model_full[rows, :].astype(F32)

    def final_one(index, carry):
        send(*final_copy(index))
        return carry
    lax.fori_loop(0, 8, final_one, 0)

    def basis_done(index, carry):
        for which in range(2):
            sent(*basis_copy(which, index // 4, index % 4))
        return carry
    lax.fori_loop(0, 24, basis_done, 0)
    for l in range(2):
        for item in init_copies(l):
            sent(*item)
        sent(*misfit_copy(l))
    for index in range(8):
        sent(*group_copy(index))
    for step in range(4):
        def z_done(s, carry):
            sent(*z_copy(step, s))
            return carry
        lax.fori_loop(0, 8, z_done, 0)
        if step % 2 == 0:
            for block in range(4):
                exchange(step, block, block).wait_send()
        else:
            for q in range(2):
                exchange(step, 2 * (1 - c) + q, q).wait_send()

    for index in range(16):
        for outer in range(2):
            sent(*spread_copy(outer, index), may_be_me=index >= 14)
    for index in range(32):
        sent(*back_copy(index), may_be_me=index == 31)

    def final_done(index, carry):
        sent(*final_copy(index))
        return carry
    lax.fori_loop(0, 8, final_done, 0)
    arrived(misfit_out, mis_r.at[0])
    arrived(estimate_out, fin_r.at[0])


def body(left_basis, right_basis, start_model, recorded, tile_ranks, mute_start, thresholds):
    def lanes(basis):
        return basis.reshape(2, 128, 2, 12, 128).transpose(0, 1, 3, 2, 4)

    wave, wave_back = wave_tables()
    anywhere = pl.BlockSpec(memory_space=pl.ANY)
    dma = pltpu.SemaphoreType.DMA
    field = jax.ShapeDtypeStruct((2, 128, 128), F32)
    return pl.pallas_call(
        kernel,
        out_shape=(field, field),
        in_specs=[anywhere] * 4 + [pl.BlockSpec(memory_space=pltpu.SMEM)] + [anywhere] * 4,
        out_specs=(anywhere, anywhere),
        scratch_shapes=[
            pltpu.VMEM((6, 512, 2, 128), BF16),
            pltpu.VMEM((6, 512, 2, 128), BF16),
            pltpu.VMEM((768, 1024), BF16),
            pltpu.VMEM((768, 1024), BF16),
            pltpu.VMEM((512, 128), BF16),
            pltpu.VMEM((2, 128, 128), F32),
            pltpu.VMEM((2, 128, 128), F32),
            pltpu.VMEM((256, 128), F32),
            pltpu.VMEM((1024, 128), BF16),
            pltpu.VMEM((256, 128), F32),
            pltpu.VMEM((4, 8, 96, 128), BF16),
            pltpu.VMEM((4, 8, 96, 128), BF16),
            pltpu.VMEM((4, 4, 128, 128), F32),
            pltpu.VMEM((4, 4, 128, 128), F32),
            pltpu.VMEM((4, 128, 128), F32),
            pltpu.VMEM((2, 2, 128, 128), BF16),
            pltpu.VMEM((2, 16, 16, 128), BF16),
            pltpu.VMEM((256, 128), F32),
            pltpu.VMEM((16, 16, 128), F32),
            pltpu.VMEM((16, 16, 128), BF16),
            pltpu.VMEM((128, 128), F32),
            pltpu.VMEM((8, 128), F32),
            pltpu.VMEM((64, 128), jnp.int32),
            pltpu.VMEM((1, 64), F32),
            pltpu.VMEM((NT, 96), BF16),
            pltpu.VMEM((64, NT), BF16),
            dma((4,)),
            pltpu.VMEM((2, 12, 128, 2, 128), BF16),
            pltpu.VMEM((2, 128, 128), F32),
            pltpu.VMEM((2, 256, 128), BF16),
            pltpu.VMEM((2, 2, 2, 384, 128), BF16),
            pltpu.VMEM((2, 4, 384, 128), BF16),
            dma((5,)), dma((8,)), dma((2,)), pltpu.SemaphoreType.REGULAR((5,)),
            dma((2, 24)), dma((2, 6)), dma((4,)), dma((2,)),
            dma((4, 8)), dma((4, 8)), dma((4, 4)), dma((4, 4)),
            dma((2, 16)), dma((2,)), dma((32,)), dma((1,)), dma((8,)), dma((1,)), dma((2,)), dma((1,)),
        ],
        compiler_params=pltpu.CompilerParams(
            collective_id=0, has_side_effects=True, vmem_limit_bytes=60 * 1024 * 1024
        ),
    )(
        lanes(left_basis), lanes(right_basis), start_model, recorded, tile_ranks,
        mute_start.T, thresholds.reshape(1, 64), jnp.asarray(wave), jnp.asarray(wave_back),
    )


def solution(mesh):
    return jax.shard_map(
        body,
        mesh=mesh,
        in_specs=(
            P("freq", "tile", None, None),
            P("freq", "tile", None, None),
            P("freq", "tile", None),
            P("freq", "tile", None),
            P(),
            P("tile", None),
            P(),
        ),
        out_specs=(P("freq", "tile", None), P("freq", "tile", None)),
        check_vma=False,
    )
```

```python
import math

import jax
import jax.numpy as jnp
import ml_dtypes
import numpy as np
from jax import lax
from jax.experimental import pallas as pl
from jax.experimental.pallas import tpu as pltpu
from jax.sharding import PartitionSpec as P

F32 = jnp.float32
BF16 = jnp.bfloat16
NT = 256
NF = 16
STEP_SIZE = 0.5
PLANE = sorted(
    ((dx, dy) for dx in range(4) for dy in range(4)),
    key=lambda o: (-min(o[0], 4 - o[0]) - min(o[1], 4 - o[1]), o),
)


def split_table(table, terms):
    parts = []
    rest = table
    for _ in range(terms):
        part = rest.astype(ml_dtypes.bfloat16)
        parts.append(part)
        rest = rest - part.astype(np.float64)
    return parts


def wave_tables():
    sample = np.arange(NT)[:, None]
    bins = np.arange(NF)[None, :] + NT // 4
    phases = (sample * bins % NT) * (2.0 * math.pi / NT)
    table = np.concatenate([np.cos(phases), -np.sin(phases)], 1)
    forward = np.concatenate(split_table(table, 3), 1)
    backward = np.concatenate(split_table(np.ascontiguousarray(table.T), 2), 0)
    return forward, backward


def kernel(
    left, right, model0, recorded, ranks, mute_in, thresholds_in, wave_in, wave_back_in,
    estimate_out, misfit_out,
    left_rows, right_rows, left_cols, right_cols,
    model_full, model_half, recorded_half, packed, weights, product,
    outbox, inbox, own_sum, sib_sum, misfit_full,
    spread_out, spread_in, spread_f32, traces, traces_b, mute_rows, window_rows,
    mute, thresholds, wave, wave_back, small_s,
    local_rows, local_model, local_weights, group_out, group_in, local_r, group_s, group_r, heard,
    basis_s, basis_r, init_s, init_r, z_s, z_r, ex_s, ex_r,
    sp_s, sp_r, back_s, back_r, fin_s, fin_r, mis_s, mis_r,
):
    freq_id = lax.axis_index("freq")
    tile_id = lax.axis_index("tile")
    x, c = freq_id // 2, freq_id % 2
    z, y = tile_id // 4, tile_id % 4
    pair = z // 8
    me = (x, c, z, y)

    def address(place):
        return (place[0] * 2 + place[1], place[2] * 4 + place[3])

    def is_me(place):
        to = address(place)
        return jnp.logical_and(to[0] == freq_id, to[1] == tile_id)

    def remote(src, dst, send_sem, recv_sem, place):
        return pltpu.make_async_remote_copy(
            src_ref=src, dst_ref=dst, send_sem=send_sem, recv_sem=recv_sem,
            device_id=address(place), device_id_type=pl.DeviceIdType.MESH,
        )

    def send(src, dst, send_sem, recv_sem, place, may_be_me=True):
        if not may_be_me:
            remote(src, dst, send_sem, recv_sem, place).start()
            return
        mine = is_me(place)

        @pl.when(jnp.logical_not(mine))
        def _():
            remote(src, dst, send_sem, recv_sem, place).start()

        @pl.when(mine)
        def _():
            pltpu.make_async_copy(src, dst, recv_sem).start()

    def sent(src, dst, send_sem, recv_sem, place, may_be_me=True):
        if not may_be_me:
            remote(src, dst, send_sem, recv_sem, place).wait_send()
            return

        @pl.when(jnp.logical_not(is_me(place)))
        def _():
            remote(src, dst, send_sem, recv_sem, place).wait_send()

    def arrived(ref, sem):
        pltpu.make_async_copy(ref, ref, sem).wait()

    barrier = pltpu.get_barrier_semaphore()

    def greet(place):
        pl.semaphore_signal(
            barrier, inc=1, device_id=address(place), device_id_type=pl.DeviceIdType.MESH
        )

    small = [
        pltpu.make_async_copy(src, dst, small_s.at[i])
        for i, (src, dst) in enumerate(
            ((mute_in, mute), (thresholds_in, thresholds), (wave_in, wave), (wave_back_in, wave_back))
        )
    ]

    local_model_copy = pltpu.make_async_copy(model0, local_model, local_r.at[4])
    local_model_copy.start()

    def local_load(h):
        for l in range(2):
            for side in range(2):
                for t3 in range(3):
                    t = 6 * side + 3 * h + t3
                    pltpu.make_async_copy(
                        right.at[l, :, t], local_rows.at[l, 3 * (2 * h + side) + t3], local_r.at[2 * h + l]
                    ).start()

    local_load(0)
    local_load(1)
    for dx, dz, dy in ((0, 0, 2), (0, 1, 0), (0, 15, 0), (1, 0, 0), (3, 0, 0), (0, 0, 1), (0, 0, 3), (0, 0, 0)):
        for dc in (1, 0):
            if (dx, dz, dy, dc) != (0, 0, 0, 0):
                greet(((x + dx) % 4, (c + dc) % 2, (z + dz) % 16, (y + dy) % 4))

    def tell(index, steps):
        for dx, dz in steps:
            pl.semaphore_signal(
                heard.at[index], inc=1, device_id=address(((x + dx) % 4, c, (z + dz) % 16, y)),
                device_id_type=pl.DeviceIdType.MESH,
            )

    def hear(index):
        pl.semaphore_wait(heard.at[index], 2)

    for copy in small:
        copy.start()

    def basis_copy(which, t, q):
        source = (right, left)[which]
        rows = (right_rows, left_rows)[which]
        side, l = q // 2, q % 2
        return (
            source.at[l, :, 6 * side + t],
            rows.at[t, pl.ds(128 * y, 128)],
            basis_s.at[which, 4 * t + q],
            basis_r.at[which, t],
            (x, side, z, 2 * c + l),
        )

    def send_basis(which, t):
        def one(q, carry):
            send(*basis_copy(which, t, q))
            return carry
        lax.fori_loop(0, 4, one, 0)

    def init_copies(l):
        place = (x, y // 2, z, 2 * c + l)
        return (
            (model0.at[l], model_half.at[y % 2], init_s.at[l], init_r.at[0], place),
            (recorded.at[l], recorded_half.at[y % 2], init_s.at[2 + l], init_r.at[1], place),
        )

    sibling = (x, 1 - c, z, y)
    lane = lax.broadcasted_iota(jnp.int32, (1, 128), 1)
    low = lane < 64
    sign = jnp.where(low, 1.0, -1.0).astype(F32)

    def interleave(values, slot):
        values = values.astype(BF16).astype(F32)
        flat = packed.reshape(1024, 128)
        flat[pl.ds(256 * slot, 128, stride=2), :] = values
        flat[pl.ds(256 * slot + 1, 128, stride=2), :] = pltpu.roll(values, 64, 1) * sign
        return flat[256 * slot:256 * slot + 256, :].astype(BF16)

    def set_weights(block, values):
        weights[256 * block:256 * block + 256, :] = interleave(values, block)

    slots = lax.broadcasted_iota(jnp.int32, (96, 128), 0)

    def z_copy(step, s):
        return (
            outbox.at[step, s], inbox.at[step, z % 8], z_s.at[step, s], z_r.at[step, z % 8],
            (x, pair, 8 * c + s, y),
        )

    def fill_outbox(step, h, values):
        for s4 in range(4):
            s = 4 * h + s4
            other = 8 * c + s
            rank = ranks[other, z] if step % 2 == 0 else ranks[z, other]
            part = values[96 * s4:96 * s4 + 96, :]
            outbox[step, s] = jnp.where(slots < rank, part, 0.0).astype(BF16)
            if step == 0:
                send(*z_copy(step, s))

    def partials(step, cols, h):
        fill_outbox(
            step, h,
            jnp.dot(cols[384 * h:384 * h + 384, :], weights[...], preferred_element_type=F32),
        )

    def group_copy(index):
        h, l, side = index // 4, (index // 2) % 2, index % 2
        return (
            group_out.at[h, l, side], group_in.at[h, y], group_s.at[index], group_r.at[h],
            (x, side, z, 2 * c + l),
        )

    def group_partials(h):
        for l in range(2):
            arrived(local_rows.at[l, pl.ds(6 * h, 6)], local_r.at[2 * h + l])
            if h == 0:
                local_weights[l] = interleave(local_model[l], l)
            view = local_rows.reshape(2, 12, 256, 128)
            def one_block(index, carry):
                rows = pl.ds(pl.multiple_of(128 * (index % 3), 128), 128)
                group_out[h, l, index // 3, rows, :] = lax.dot_general(
                    view[l, 6 * h + index], local_weights[l],
                    (((0,), (0,)), ((), ())), preferred_element_type=F32,
                ).astype(BF16)
                return carry
            for index in range(6):
                one_block(index, 0)

    def send_line(step):
        place = z % 8
        upper = place // 4
        reach = upper * (7 - place) + (1 - upper) * place
        same = 1 - (pair + c) % 2
        for k in range(8):
            n = k + same * (7 - 2 * k)
            inside = (2 * reach - n + 8) // 8
            both = ((n + 1) // 2) * (2 * (n % 2) - 1)
            one = (n - reach) * (1 - 2 * upper)
            s = place + inside * both + (1 - inside) * one
            send(*z_copy(step, s), may_be_me=k == 7)

    def transpose(rows, cols, t):
        cols[pl.ds(pl.multiple_of(128 * t, 128), 128), :] = rows.reshape(6, 1024, 128)[t].T

    def expand(rows, step, block, slot):
        start = 256 * block if isinstance(block, int) else pl.multiple_of(256 * block, 256)
        view = rows.reshape(6, 1024, 128)
        lhs = jnp.concatenate([view[t, pl.ds(start, 256), :] for t in range(6)], 1)
        rhs = inbox[step].reshape(768, 128)
        flat = product.reshape(1024, 128)
        flat[256 * slot:256 * slot + 256, :] = jnp.dot(lhs, rhs, preferred_element_type=F32)
        real = flat[pl.ds(256 * slot, 128, stride=2), :]
        imag = flat[pl.ds(256 * slot + 1, 128, stride=2), :]
        return real - pltpu.roll(imag, 64, 1) * sign

    def exchange(step, block, slot):
        return remote(
            own_sum.at[step, block], sib_sum.at[step, slot], ex_s.at[step, slot],
            ex_r.at[step, slot], sibling,
        )

    def receive_line(step):
        for s in range(8):
            arrived(inbox.at[step, s], z_r.at[step, s])

    def residual(step):
        receive_line(step)
        for block in range(4):
            part = expand(left_rows, step, block, block)
            kept = jnp.where(block // 2 == c, recorded_half[block % 2], 0.0)
            own_sum[step, block] = part - kept
            exchange(step, block, block).start()
        for block in range(4):
            exchange(step, block, block).wait_recv()
            values = own_sum[step, block] + sib_sum[step, block]
            if step == 2:
                misfit_full[block] = values
            set_weights(block, values)

    def update(step):
        receive_line(step)
        for q in range(2):
            block = 2 * (1 - c) + q
            own_sum[step, block] = expand(right_rows, step, block, q)
            exchange(step, block, q).start()
        for q in range(2):
            own_sum[step, 2 * c + q] = expand(right_rows, step, 2 * c + q, 2 + q)
        if step == 1:
            arrived(model_half, init_r.at[0])
        for q in range(2):
            exchange(step, 2 * (1 - c) + q, q).wait_recv()
            total = own_sum[step, 2 * c + q] + sib_sum[step, q]
            model_half[q] = model_half[q] - STEP_SIZE * total

    SPREAD = [(dx, dc, q) for dx in (2, 1, 3, 0) for dc in (1, 0) for q in range(2)]

    def spread_copy(outer, index):
        dx, dc, q = SPREAD[index]
        column, core = (x + dx) % 4, (c + dc) % 2
        return (
            spread_out.at[outer, q, pl.ds(pl.multiple_of(32 * column + 16 * core, 16), 16)],
            spread_in.at[outer, 4 * x + y],
            sp_s.at[outer, index], sp_r.at[outer],
            (column, core, z, 2 * c + q),
        )

    def sparsify(outer):
        spread_out[outer] = model_half[...].astype(BF16)

        for index in range(16):
            send(*spread_copy(outer, index), may_be_me=index >= 14)
        arrived(spread_in.at[outer], sp_r.at[outer])
        spread_f32[...] = spread_in[outer].reshape(256, 128).astype(F32)
        flat = traces.reshape(256, 128)
        sample = lax.broadcasted_iota(jnp.int32, (NT, 128), 0).astype(F32)

        def one_pair(p, carry):
            even = spread_f32[pl.ds(2 * p, 16, stride=16), :]
            odd = spread_f32[pl.ds(2 * p + 1, 16, stride=16), :]
            real = jnp.where(low, even, pltpu.roll(odd, 64, 1))
            imag = jnp.where(low, pltpu.roll(even, 64, 1), odd)
            both = jnp.concatenate([real, imag], 0).astype(BF16)
            series = jnp.dot(
                wave[...], jnp.concatenate([both, both, both], 0), preferred_element_type=F32
            ) * (1.0 / math.sqrt(NF))
            series = jnp.where(sample >= window_rows[p:p + 1, :], series, 0.0)
            series = series - jnp.clip(series, -cutoff, cutoff)
            high = series.astype(BF16)
            rest = (series - high.astype(F32)).astype(BF16)
            first = jnp.dot(wave_back[...], high, preferred_element_type=F32)
            second = jnp.dot(wave_back[0:32, :], rest, preferred_element_type=F32)
            returned = (first[0:32] + first[32:64] + second) * (2.0 * math.sqrt(NF) / NT)
            real, imag = returned[0:16], returned[16:32]
            flat[pl.ds(2 * p, 16, stride=16), :] = jnp.where(low, real, pltpu.roll(imag, 64, 1))
            flat[pl.ds(2 * p + 1, 16, stride=16), :] = jnp.where(low, pltpu.roll(real, 64, 1), imag)
            return carry
        for p in range(8):
            one_pair(p, 0)

    BACK = [(dx, dy, dc) for dx, dy in PLANE for dc in (1, 0)]

    def back_copy(index):
        dx, dy, dc = BACK[index]
        column, row, core = (x + dx) % 4, (y + dy) % 4, (c + dc) % 2
        return (
            traces_b.at[4 * column + row],
            model_full.at[pl.ds(pl.multiple_of(128 * y + 32 * x + 16 * c, 16), 16)],
            back_s.at[index], back_r.at[0],
            (column, core, z, row),
        )

    def final_copy(index):
        return (
            traces.at[pl.ds(2 * index, 2)],
            estimate_out.at[:, pl.ds(pl.multiple_of(32 * x + 16 * c, 16), 16)],
            fin_s.at[index], fin_r.at[0],
            (index // 2, index % 2, z, y),
        )

    def misfit_copy(q):
        return (
            misfit_full.at[2 * c + q], misfit_out.at[y % 2], mis_s.at[q], mis_r.at[0],
            (x, y // 2, z, 2 * c + q),
        )

    local_model_copy.wait()
    group_partials(0)
    pl.semaphore_wait(barrier, 15)
    for index in range(4):
        send(*group_copy(index))
    tell(0, ((0, 1), (0, 15)))
    tell(3, ((1, 0), (3, 0)))
    group_partials(1)
    for index in range(4, 8):
        send(*group_copy(index))
    for t in range(2):
        send_basis(1, t)
    hear(0)
    tell(1, ((0, 2), (0, 14)))
    hear(1)
    tell(2, ((0, 4), (0, 12)))
    hear(3)
    tell(4, ((1, 0), (3, 0)))
    hear(2)
    hear(4)
    for h in range(2):
        arrived(group_in.at[h], group_r.at[h])
        total = group_in[h, 0].astype(F32)
        for g in range(1, 4):
            total = total + group_in[h, g].astype(F32)
        fill_outbox(0, h, total)
        for t in range(2 * h + 2, 2 * h + 4):
            send_basis(1, t)
    for l in range(2):
        send(*init_copies(l)[1])
    for copy in small:
        copy.wait()

    mute_t = mute[...].astype(F32).T
    mute_rows[...] = jnp.concatenate([mute_t, mute_t], 1)
    first_row = pl.multiple_of(32 * x + 16 * c, 16)
    window_rows[...] = jnp.where(
        low, mute_rows[pl.ds(first_row, 8, stride=2), :], mute_rows[pl.ds(first_row + 1, 8, stride=2), :]
    )
    cutoff = jnp.concatenate([thresholds[...], thresholds[...]], 1)

    def left_block(t, carry):
        arrived(left_rows.at[t], basis_r.at[1, t])
        send_basis(0, t)
        transpose(left_rows, left_cols, t)
        return carry
    lax.fori_loop(0, 6, left_block, 0)
    for l in range(2):
        send(*init_copies(l)[0])
    arrived(recorded_half, init_r.at[1])

    for outer in range(2):
        if outer == 1:
            partials(2, right_cols, 0)
            partials(2, right_cols, 1)
            send_line(2)
        residual(2 * outer)
        partials(2 * outer + 1, left_cols, 0)
        partials(2 * outer + 1, left_cols, 1)
        send_line(2 * outer + 1)
        if outer == 1:
            for q in range(2):
                send(*misfit_copy(q))
        else:
            def right_block(t, carry):
                arrived(right_rows.at[t], basis_r.at[0, t])
                transpose(right_rows, right_cols, t)
                return carry
            lax.fori_loop(0, 6, right_block, 0)
        update(2 * outer + 1)
        sparsify(outer)
        if outer == 0:
            traces_b[...] = traces[...].astype(BF16)

            for index in range(32):
                send(*back_copy(index), may_be_me=index == 31)
            arrived(model_full, back_r.at[0])
            for block in range(4):
                set_weights(block, model_full[128 * block:128 * block + 128, :].astype(F32))
            for q in range(2):
                rows = pl.ds(pl.multiple_of(256 * c + 128 * q, 128), 128)
                model_half[q] = model_full[rows, :].astype(F32)

    def final_one(index, carry):
        send(*final_copy(index))
        return carry
    lax.fori_loop(0, 8, final_one, 0)

    def basis_done(index, carry):
        for which in range(2):
            sent(*basis_copy(which, index // 4, index % 4))
        return carry
    lax.fori_loop(0, 24, basis_done, 0)
    for l in range(2):
        for item in init_copies(l):
            sent(*item)
        sent(*misfit_copy(l))
    for index in range(8):
        sent(*group_copy(index))
    for step in range(4):
        def z_done(s, carry):
            sent(*z_copy(step, s))
            return carry
        lax.fori_loop(0, 8, z_done, 0)
        if step % 2 == 0:
            for block in range(4):
                exchange(step, block, block).wait_send()
        else:
            for q in range(2):
                exchange(step, 2 * (1 - c) + q, q).wait_send()

    for index in range(16):
        for outer in range(2):
            sent(*spread_copy(outer, index), may_be_me=index >= 14)
    for index in range(32):
        sent(*back_copy(index), may_be_me=index == 31)

    def final_done(index, carry):
        sent(*final_copy(index))
        return carry
    lax.fori_loop(0, 8, final_done, 0)
    arrived(misfit_out, mis_r.at[0])
    arrived(estimate_out, fin_r.at[0])


def body(left_basis, right_basis, start_model, recorded, tile_ranks, mute_start, thresholds):
    def lanes(basis):
        return basis.reshape(2, 128, 2, 12, 128).transpose(0, 1, 3, 2, 4)

    wave, wave_back = wave_tables()
    anywhere = pl.BlockSpec(memory_space=pl.ANY)
    dma = pltpu.SemaphoreType.DMA
    field = jax.ShapeDtypeStruct((2, 128, 128), F32)
    return pl.pallas_call(
        kernel,
        out_shape=(field, field),
        in_specs=[anywhere] * 4 + [pl.BlockSpec(memory_space=pltpu.SMEM)] + [anywhere] * 4,
        out_specs=(anywhere, anywhere),
        scratch_shapes=[
            pltpu.VMEM((6, 512, 2, 128), BF16),
            pltpu.VMEM((6, 512, 2, 128), BF16),
            pltpu.VMEM((768, 1024), BF16),
            pltpu.VMEM((768, 1024), BF16),
            pltpu.VMEM((512, 128), BF16),
            pltpu.VMEM((2, 128, 128), F32),
            pltpu.VMEM((2, 128, 128), F32),
            pltpu.VMEM((4, 256, 128), F32),
            pltpu.VMEM((1024, 128), BF16),
            pltpu.VMEM((4, 256, 128), F32),
            pltpu.VMEM((4, 8, 96, 128), BF16),
            pltpu.VMEM((4, 8, 96, 128), BF16),
            pltpu.VMEM((4, 4, 128, 128), F32),
            pltpu.VMEM((4, 4, 128, 128), F32),
            pltpu.VMEM((4, 128, 128), F32),
            pltpu.VMEM((2, 2, 128, 128), BF16),
            pltpu.VMEM((2, 16, 16, 128), BF16),
            pltpu.VMEM((256, 128), F32),
            pltpu.VMEM((16, 16, 128), F32),
            pltpu.VMEM((16, 16, 128), BF16),
            pltpu.VMEM((128, 128), F32),
            pltpu.VMEM((8, 128), F32),
            pltpu.VMEM((64, 128), jnp.int32),
            pltpu.VMEM((1, 64), F32),
            pltpu.VMEM((NT, 96), BF16),
            pltpu.VMEM((64, NT), BF16),
            dma((4,)),
            pltpu.VMEM((2, 12, 128, 2, 128), BF16),
            pltpu.VMEM((2, 128, 128), F32),
            pltpu.VMEM((2, 256, 128), BF16),
            pltpu.VMEM((2, 2, 2, 384, 128), BF16),
            pltpu.VMEM((2, 4, 384, 128), BF16),
            dma((5,)), dma((8,)), dma((2,)), pltpu.SemaphoreType.REGULAR((5,)),
            dma((2, 24)), dma((2, 6)), dma((4,)), dma((2,)),
            dma((4, 8)), dma((4, 8)), dma((4, 4)), dma((4, 4)),
            dma((2, 16)), dma((2,)), dma((32,)), dma((1,)), dma((8,)), dma((1,)), dma((2,)), dma((1,)),
        ],
        compiler_params=pltpu.CompilerParams(
            collective_id=0, has_side_effects=True, vmem_limit_bytes=60 * 1024 * 1024
        ),
    )(
        lanes(left_basis), lanes(right_basis), start_model, recorded, tile_ranks,
        mute_start.T, thresholds.reshape(1, 64), jnp.asarray(wave), jnp.asarray(wave_back),
    )


def solution(mesh):
    return jax.shard_map(
        body,
        mesh=mesh,
        in_specs=(
            P("freq", "tile", None, None),
            P("freq", "tile", None, None),
            P("freq", "tile", None),
            P("freq", "tile", None),
            P(),
            P("tile", None),
            P(),
        ),
        out_specs=(P("freq", "tile", None), P("freq", "tile", None)),
        check_vma=False,
    )
```
